128 devices in a mesh: wide: 32 (over x_lo, z, y), narrow: 4 (over x_hi, core).
Axes of the slice: x: 4 (x_hi: 2, x_lo: 2; x = x_hi * 2 + x_lo), y: 4, z: 4, core: 2. Of those that a mesh axis runs over, the one named last changes fastest.
Arguments:
- activations: bfloat16 [512, 8192], P(('wide', 'narrow')), may hold values from -6 to 6
- cotangent: bfloat16 [512, 8192], P('wide', 'narrow'), may hold values from -6 to 6
- gate_proj: bfloat16 [8192, 26624], P('narrow', 'wide'), may hold values from -0.0625 to 0.0625
- up_proj: bfloat16 [8192, 26624], P('narrow', 'wide'), may hold values from -0.0625 to 0.0625
- down_proj: bfloat16 [26624, 8192], P('wide', 'narrow'), may hold values from -0.0390625 to 0.0390625
Outputs:
- block_output: bfloat16 [512, 8192], P('wide', 'narrow')
- input_gradient: bfloat16 [512, 8192], P(('wide', 'narrow'))
- gate_gradient: bfloat16 [8192, 26624], P('narrow', 'wide')
- up_gradient: bfloat16 [8192, 26624], P('narrow', 'wide')
- down_gradient: bfloat16 [26624, 8192], P('wide', 'narrow')
The draws below stay inside these ranges and needn't reach their ends.
All inputs are finite; a program needn't handle non-finite values.
Results may differ from the reference program's by a relative error of at most 0.005.
Values may be sent and summed in bfloat16 or wider, within the bound.
A program may use at most 128 MiB of HBM per device.

```python
import jax
import jax.numpy as jnp

D = 8192
FF = 26624
TOKENS = 512


def steps_of(key, dims, split, smallest, high):
    def one(axis_at, parts):
        steps = jax.random.uniform(jax.random.fold_in(jax.random.fold_in(key, 6), axis_at), (parts,), jnp.float32, smallest / len(split), high / len(split))
        return jnp.repeat(jnp.exp(steps), dims[axis_at] // parts).reshape((-1,) + (1,) * (len(dims) - axis_at - 1))

    level = one(*split[0])
    for cut in split[1:]:
        level = level * one(*cut)
    return level


def noise(rng, extent, deviation, reach, cuts=(), dtype=jnp.bfloat16):
    values = jax.random.normal(rng, extent, jnp.float32) * deviation
    if len(cuts) > 0:
        values = steps_of(rng, extent, cuts, -0.22, 0.18) * values
    return jnp.clip(values, min=-reach, max=reach).astype(dtype)


def setup_inputs(seed: int = 0) -> dict:
    seeds = jax.random.split(jax.random.key(seed), 6)
    activations = noise(seeds[0], (TOKENS, D), 1.0, 6.0, ((0, 128),))
    cotangent = noise(seeds[1], (TOKENS, D), 1.0, 6.0, ((0, 32), (1, 4)))
    gate_proj = noise(seeds[2], (D, FF), D ** -0.5, 0.0625, ((0, 4), (1, 32)))
    up_proj = noise(seeds[3], (D, FF), D ** -0.5, 0.0625, ((0, 4), (1, 32)))
    down_proj = noise(seeds[4], (FF, D), FF ** -0.5, 0.0390625, ((0, 32), (1, 4)))
    return dict(activations=activations, cotangent=cotangent, gate_proj=gate_proj, up_proj=up_proj, down_proj=down_proj)


def silu_parts(gate):
    sigma = jax.nn.sigmoid(gate)
    return gate * sigma, sigma * (1.0 + gate * (1.0 - sigma))


def reference(activations, cotangent, gate_proj, up_proj, down_proj):
    gate = jnp.dot(activations, gate_proj, preferred_element_type=jnp.float32)
    up = jnp.dot(activations, up_proj, preferred_element_type=jnp.float32)
    active, slope = silu_parts(gate)
    hidden = (active * up).astype(jnp.bfloat16)
    block_output = jnp.dot(hidden, down_proj, preferred_element_type=jnp.float32).astype(jnp.bfloat16)
    back = jnp.dot(cotangent, down_proj.T, preferred_element_type=jnp.float32)
    gate_delta = (back * up * slope).astype(jnp.bfloat16)
    up_delta = (back * active).astype(jnp.bfloat16)
    down_gradient = jnp.dot(hidden.T, cotangent, preferred_element_type=jnp.float32).astype(jnp.bfloat16)
    gate_gradient = jnp.dot(activations.T, gate_delta, preferred_element_type=jnp.float32).astype(jnp.bfloat16)
    up_gradient = jnp.dot(activations.T, up_delta, preferred_element_type=jnp.float32).astype(jnp.bfloat16)
    input_gradient = (jnp.dot(gate_delta, gate_proj.T, preferred_element_type=jnp.float32)
                      + jnp.dot(up_delta, up_proj.T, preferred_element_type=jnp.float32)).astype(jnp.bfloat16)
    return block_output, input_gradient, gate_gradient, up_gradient, down_gradient
```

```python
import jax
import jax.numpy as jnp
from jax import lax
from jax.experimental import pallas as pl
from jax.experimental.pallas import tpu as pltpu
from jax.sharding import PartitionSpec as P

MESH = pl.DeviceIdType.MESH
BF = jnp.bfloat16
F32 = jnp.float32

XL, Z, Y = 2, 4, 4
ROWS = 16
TILE = 2048
HALF = TILE // 2
FFL = 832
QUART = 64
STEP = 512


def dot(a, b):
    return lax.dot_general(a, b, (((1,), (0,)), ((), ())), preferred_element_type=F32)


def dot_t(a, b):
    return lax.dot_general(a, b, (((1,), (1,)), ((), ())), preferred_element_type=F32)


def kernel(
    act, cot, wg_hbm, wu_hbm, wd_hbm,
    out_ref, ig_ref, f_hbm, c_hbm, h_hbm, gd_hbm, ud_hbm,
    wg, wu, wd, feat, cota, a_send, a_recv, a_f32,
    g_send, g_own, g_recv, x_send, x_recv, hd,
    part, r1_send, r1_recv, s1, r2_send, r2_recv, xo_send, xo_recv, t_f32, o_f32, n_send, n_recv,
    w_sem, o_sem, a_ss, a_rs, cx_ss, cx_rs, p1_ss, p1_rs, p2_ss, p2_rs,
    g_ss, g_rs, x_ss, x_rs, h_ss, h_rs, r1_ss, r1_rs, r2_ss, r2_rs, xo_ss, xo_rs, n_ss, n_rs,
):
    w = lax.axis_index("wide")
    n = lax.axis_index("narrow")
    y = lax.rem(w, Y)
    z = lax.rem(w // Y, Z)
    xl = w // (Y * Z)
    xh = n // 2
    core = lax.rem(n, 2)
    quarter = core * 2 + xh
    far_quarter = core * 2 + (1 - xh)

    def wide_id(a, b, c):
        return (a * Z + b) * Y + c

    def y_dev(d):
        return (wide_id(xl, z, lax.rem(y + d, Y)), n)

    def z_dev(d):
        return (wide_id(xl, lax.rem(z + d, Z), y), n)

    def line_dev(dx, dn):
        return (wide_id(lax.rem(xl + dx, XL), z, y), lax.rem(n + dn, 4))

    sibling = (w, xh * 2 + (1 - core))
    across = (w, (1 - xh) * 2 + core)
    peer = (wide_id(1 - xl, z, y), n)
    line = [(dx, dn) for dx in range(XL) for dn in range(4) if (dx, dn) != (0, 0)]

    sends = []

    def remote(src, dst, ss, rs, dev):
        return pltpu.make_async_remote_copy(
            src_ref=src, dst_ref=dst, send_sem=ss, recv_sem=rs, device_id=dev, device_id_type=MESH
        )

    def send(src, dst, ss, rs, dev):
        copy = remote(src, dst, ss, rs, dev)
        copy.start()
        sends.append(copy)

    def landed(dst, ss, rs, dev):
        remote(dst, dst, ss, rs, dev).wait_recv()

    loads = [
        pltpu.make_async_copy(src, dst, w_sem.at[i])
        for i, (src, dst) in enumerate(((wg_hbm, wg), (wu_hbm, wu), (wd_hbm, wd)))
    ]
    for load in loads:
        load.start()

    barrier = pltpu.get_barrier_semaphore()
    friends = [y_dev(d) for d in (1, 2, 3)] + [z_dev(d) for d in (1, 2, 3)] + [line_dev(*k) for k in line]
    for dev in friends:
        pl.semaphore_signal(barrier, inc=1, device_id=dev, device_id_type=MESH)

    rows4 = act[...].astype(F32)
    for m in range(4):
        for k in range(4):
            at = m * TILE + k * STEP
            t_f32[m, pl.ds(4 * k, 4), :] = rows4[:, at : at + STEP]
    for m in range(4):
        a_send[m] = t_f32[m].astype(BF)
    cota[xl, z, y] = cot[...]

    pl.semaphore_wait(barrier, len(friends))

    here = xl * 4 + n
    for i, (dx, dn) in enumerate(line):
        m = lax.rem(n + dn, 4)
        send(a_send.at[m], a_recv.at[here], a_ss.at[i], a_rs.at[i], line_dev(dx, dn))
    send(cota.at[xl, z, y], cota.at[xl, z, y], cx_ss, cx_rs, peer)
    a_recv[here] = a_send[n]
    for i, (dx, dn) in enumerate(line):
        src = lax.rem(xl + dx, XL) * 4 + lax.rem(n + 4 - dn, 4)
        landed(a_recv.at[src], a_ss.at[i], a_rs.at[i], line_dev(dx, dn))
    for s in range(8):
        t_f32[s] = a_recv[s].astype(F32)
        for k in range(4):
            a_f32[s // 4, pl.ds(4 * (s % 4), 4), pl.ds(k * STEP, STEP)] = t_f32[s, pl.ds(4 * k, 4), :]
    for c in range(XL):
        feat[c, z, y] = a_f32[c].astype(BF)

    bufs = (feat, cota)
    cols = (pl.ds(0, HALF), pl.ds(HALF, HALF))

    def gather1(b, c):
        block = [bufs[b].at[c, z, y, :, cols[h]] for h in (0, 1)]
        for d in (1, 2, 3):
            send(block[0], block[0], p1_ss.at[b, c, 0, d - 1], p1_rs.at[b, c, 0, d - 1], z_dev(d))
            send(block[1], block[1], p1_ss.at[b, c, 1, d - 1], p1_rs.at[b, c, 1, d - 1], y_dev(d))

    def gather1_wait(b, c):
        for d in (1, 2, 3):
            landed(bufs[b].at[c, lax.rem(z + 4 - d, Z), y, :, cols[0]], p1_ss.at[b, c, 0, d - 1], p1_rs.at[b, c, 0, d - 1], z_dev(d))
            landed(bufs[b].at[c, z, lax.rem(y + 4 - d, Y), :, cols[1]], p1_ss.at[b, c, 1, d - 1], p1_rs.at[b, c, 1, d - 1], y_dev(d))

    low, high = pl.ds(0, 2), pl.ds(2, 2)

    def ring_block(b, c, h, back, part_of):
        if h == 0:
            return bufs[b].at[c, part_of, lax.rem(y + 4 - back, Y), :, cols[0]]
        return bufs[b].at[c, lax.rem(z + 4 - back, Z), part_of, :, cols[1]]

    def ring_dev(h, d):
        return y_dev(d) if h == 0 else z_dev(d)

    def gather2(b, c):
        for i, (d, part_of) in enumerate(((1, low), (3, high), (1, high), (3, low))):
            for h in (0, 1):
                block = ring_block(b, c, h, 0, part_of)
                send(block, block, p2_ss.at[b, c, h, i], p2_rs.at[b, c, h, i], ring_dev(h, d))

    def gather2_pass_on(b, c):
        for i, (d, part_of) in enumerate(((1, low), (3, high))):
            for h in (0, 1):
                block = ring_block(b, c, h, d, part_of)
                landed(block, p2_ss.at[b, c, h, i], p2_rs.at[b, c, h, i], ring_dev(h, d))
                send(block, block, p2_ss.at[b, c, h, 4 + i], p2_rs.at[b, c, h, 4 + i], ring_dev(h, d))

    def gather2_wait(b, c):
        for i, (d, back, part_of) in ((2, (1, 1, high)), (3, (3, 3, low)), (4, (1, 2, low)), (5, (3, 2, high))):
            for h in (0, 1):
                landed(ring_block(b, c, h, back, part_of), p2_ss.at[b, c, h, i], p2_rs.at[b, c, h, i], ring_dev(h, d))

    def partial(c, half, ks, into):
        for k in ks:
            if k == 2:
                v = dot_t(cota[c, pl.ds(2 * half, 2)].reshape(2 * QUART, TILE), wd[...])
            else:
                v = dot_t(feat[c, pl.ds(2 * half, 2)].reshape(2 * QUART, TILE), (wg, wu)[k][...])
            into[c, k] = v.reshape(2, QUART, FFL)

    groups = ((0, 2), (2, 1))

    def sum_send(c, g):
        first, count = groups[g]
        partial(c, 1 - core, range(first, first + count), g_send)
        ks = pl.ds(first, count)
        send(g_send.at[c, ks], g_recv.at[c, ks], g_ss.at[c, g], g_rs.at[c, g], sibling)

    def sum_own(c, g):
        first, count = groups[g]
        partial(c, core, range(first, first + count), g_own)

    def sum_across(c, g):
        first, count = groups[g]
        ks = pl.ds(first, count)
        landed(g_recv.at[c, ks], g_ss.at[c, g], g_rs.at[c, g], sibling)
        for k in range(first, first + count):
            x_send[c, k] = (g_own[c, k, 1 - xh] + g_recv[c, k, 1 - xh]).astype(BF)
        send(x_send.at[c, ks], x_recv.at[c, ks], x_ss.at[c, g], x_rs.at[c, g], across)

    def total(c, k):
        return g_own[c, k, xh] + g_recv[c, k, xh] + x_recv[c, k].astype(F32)

    def spread(c, g):
        ks = pl.ds(*((0, 1), (1, 2))[g])
        block = hd.at[ks, c, quarter]
        send(block, block, h_ss.at[c, g, 0], h_rs.at[c, g, 0], across)
        send(block, block, h_ss.at[c, g, 1], h_rs.at[c, g, 1], sibling)

    def spread_pass_on(c, g):
        ks = pl.ds(*((0, 1), (1, 2))[g])
        block = hd.at[ks, c, far_quarter]
        landed(block, h_ss.at[c, g, 0], h_rs.at[c, g, 0], across)
        send(block, block, h_ss.at[c, g, 2], h_rs.at[c, g, 2], sibling)

    def spread_wait(c, g):
        ks = pl.ds(*((0, 1), (1, 2))[g])
        other = (1 - core) * 2
        landed(hd.at[ks, c, other + xh], h_ss.at[c, g, 1], h_rs.at[c, g, 1], sibling)
        landed(hd.at[ks, c, other + 1 - xh], h_ss.at[c, g, 2], h_rs.at[c, g, 2], sibling)

    def hidden(c):
        landed(x_recv.at[c, pl.ds(0, 2)], x_ss.at[c, 0], x_rs.at[c, 0], across)
        gate, up = total(c, 0), total(c, 1)
        hd[0, c, quarter] = (gate * lax.logistic(gate) * up).astype(BF)
        spread(c, 0)

    def deltas(c):
        landed(x_recv.at[c, pl.ds(2, 1)], x_ss.at[c, 1], x_rs.at[c, 1], across)
        gate, up, back = total(c, 0), total(c, 1), total(c, 2)
        sigma = lax.logistic(gate)
        hd[1, c, quarter] = (back * up * (sigma * (1.0 + gate * (1.0 - sigma)))).astype(BF)
        hd[2, c, quarter] = (back * (gate * sigma)).astype(BF)
        spread(c, 1)

    def product(k, c):
        def columns(j, carry):
            at = pl.ds(pl.multiple_of(j * STEP, STEP), STEP)
            if k == 0:
                v = dot(hd[0, c].reshape(4 * QUART, FFL), wd[:, at])
            else:
                v = dot(hd[1, c].reshape(4 * QUART, FFL), wg[:, at])
                v += dot(hd[2, c].reshape(4 * QUART, FFL), wu[:, at])
            v = v.reshape(Z, Y, ROWS, STEP)
            part[k, c, :, :, :, at] = v
            r1_send[k, c, :, :, :, at] = v.astype(BF)
            return carry

        lax.fori_loop(0, TILE // STEP, columns, 0)
        for d in (1, 2, 3):
            send(r1_send.at[k, c, :, lax.rem(y + d, Y), :, cols[0]], r1_recv.at[k, c, 0, d - 1], r1_ss.at[k, c, 0, d - 1], r1_rs.at[k, c, 0, d - 1], y_dev(d))
            send(r1_send.at[k, c, lax.rem(z + d, Z), :, :, cols[1]], r1_recv.at[k, c, 1, d - 1], r1_ss.at[k, c, 1, d - 1], r1_rs.at[k, c, 1, d - 1], z_dev(d))

    def scatter2(k, c):
        for h in (0, 1):
            for d in (1, 2, 3):
                landed(r1_recv.at[k, c, h, d - 1], r1_ss.at[k, c, h, d - 1], r1_rs.at[k, c, h, d - 1], ring_dev(h, d))
            own = part[k, c, :, y, :, cols[0]] if h == 0 else part[k, c, z, :, :, cols[1]]
            for d in (1, 2, 3):
                own += r1_recv[k, c, h, d - 1].astype(F32)
            s1[k, c, h] = own
            r2_send[k, c, h] = own.astype(BF)
            for d in (1, 2, 3):
                to = lax.rem((z if h == 0 else y) + d, 4)
                send(r2_send.at[k, c, h, to], r2_recv.at[k, c, h, d - 1], r2_ss.at[k, c, h, d - 1], r2_rs.at[k, c, h, d - 1], ring_dev(1 - h, d))

    def scattered(k, c):
        for h in (0, 1):
            for d in (1, 2, 3):
                landed(r2_recv.at[k, c, h, d - 1], r2_ss.at[k, c, h, d - 1], r2_rs.at[k, c, h, d - 1], ring_dev(1 - h, d))
            own = s1[k, c, h, z if h == 0 else y]
            for d in (1, 2, 3):
                own += r2_recv[k, c, h, d - 1].astype(F32)
            xo_send[k, c, :, cols[h]] = own

    def output_peer(c):
        copy = remote(xo_send.at[0, c], xo_recv, xo_ss, xo_rs, peer)
        pl.when(xl != c)(copy.start)

    def owners(c):
        for m in range(4):
            for k in range(4):
                t_f32[m, pl.ds(4 * k, 4), :] = xo_send[1, c, pl.ds(4 * m, 4), pl.ds(k * STEP, STEP)]
        for m in range(4):
            n_send[c, m] = t_f32[m].astype(BF)
        dx = lax.rem(c + 2 - xl, XL)
        for dn in range(4):
            m = lax.rem(n + dn, 4)
            copy = remote(n_send.at[c, m], n_recv.at[here], n_ss.at[c, dn], n_rs.at[dx, dn], (wide_id(c, z, y), m))
            if dn == 0:
                pl.when(xl != c)(copy.start)
            else:
                copy.start()
                sends.append(copy)

    for b, c in ((0, 0), (0, 1)):
        gather1(b, c)
    landed(cota.at[1 - xl, z, y], cx_ss, cx_rs, peer)
    gather1(1, 0)
    gather1_wait(0, 0)
    gather2(0, 0)
    gather1(1, 1)
    gather1_wait(1, 0)
    gather2_pass_on(0, 0)
    gather2(1, 0)
    for load in loads:
        load.wait()
    gather2_wait(0, 0)
    sum_send(0, 0)
    gather2_pass_on(1, 0)
    gather1_wait(0, 1)
    gather2(0, 1)
    sum_own(0, 0)
    sum_across(0, 0)
    gather2_wait(1, 0)
    gather2_pass_on(0, 1)
    gather1_wait(1, 1)
    gather2(1, 1)
    sum_send(0, 1)
    sum_own(0, 1)
    sum_across(0, 1)
    gather2_wait(0, 1)
    gather2_pass_on(1, 1)
    sum_send(1, 0)
    sum_own(1, 0)
    hidden(0)
    sum_across(1, 0)
    deltas(0)
    gather2_wait(1, 1)
    stores = [
        pltpu.make_async_copy(feat, f_hbm, o_sem.at[0]),
        pltpu.make_async_copy(cota, c_hbm, o_sem.at[1]),
    ]
    for store in stores:
        store.start()
    sum_send(1, 1)
    sum_own(1, 1)
    sum_across(1, 1)
    spread_pass_on(0, 0)
    spread_wait(0, 0)
    product(0, 0)
    spread_pass_on(0, 1)
    hidden(1)
    spread_wait(0, 1)
    product(1, 0)
    deltas(1)
    scatter2(0, 0)
    spread_pass_on(1, 0)
    spread_wait(1, 0)
    product(0, 1)
    scatter2(1, 0)
    spread_pass_on(1, 1)
    spread_wait(1, 1)
    product(1, 1)
    for k in range(3):
        stores.append(pltpu.make_async_copy(hd.at[k], (h_hbm, gd_hbm, ud_hbm)[k], o_sem.at[2 + k]))
        stores[-1].start()
    scattered(0, 0)
    output_peer(0)
    scatter2(0, 1)
    scattered(1, 0)
    owners(0)
    scatter2(1, 1)
    scattered(0, 1)
    output_peer(1)
    scattered(1, 1)
    owners(1)
    landed(xo_recv, xo_ss, xo_rs, peer)
    out_ref[...] = (xo_send[0, xl] + xo_recv[...]).astype(BF)
    n_recv[here] = n_send[xl, n]
    for dx, dn in line:
        src = lax.rem(xl + dx, XL) * 4 + lax.rem(n + 4 - dn, 4)
        landed(n_recv.at[src], n_ss.at[0, 0], n_rs.at[dx, dn], line_dev(dx, dn))
    for m in range(4):
        t_f32[m] = n_recv[m].astype(F32) + n_recv[4 + m].astype(F32)
        for k in range(4):
            at = m * TILE + k * STEP
            o_f32[:, pl.ds(at, STEP)] = t_f32[m, pl.ds(4 * k, 4), :]
    ig_ref[...] = o_f32[...].astype(BF)

    for copy in sends:
        copy.wait_send()
    remote(xo_send.at[0, 1 - xl], xo_recv, xo_ss, xo_rs, peer).wait_send()
    remote(n_send.at[1 - xl, n], n_recv.at[here], n_ss.at[1 - xl, 0], n_rs.at[1, 0], peer).wait_send()
    for store in stores:
        store.wait()


def forward_backward(act, cot, gate_proj, up_proj, down_proj):
    any_space = pl.BlockSpec(memory_space=pl.ANY)
    vmem = pl.BlockSpec(memory_space=pltpu.VMEM)
    sem = pltpu.SemaphoreType.DMA
    rows = (XL, Z, Y, ROWS, TILE)
    units = (XL, 4, QUART, FFL)
    like = jax.ShapeDtypeStruct
    flops = 2 * 6 * XL * Z * Y * ROWS * TILE * FFL
    return pl.pallas_call(
        kernel,
        name="ffn",
        out_shape=[
            like((ROWS, TILE), BF), like((4, 4 * TILE), BF),
            like(rows, BF), like(rows, BF), like(units, BF), like(units, BF), like(units, BF),
        ],
        in_specs=[vmem, vmem, any_space, any_space, any_space],
        out_specs=[vmem, vmem] + [any_space] * 5,
        scratch_shapes=[
            pltpu.VMEM((FFL, TILE), BF), pltpu.VMEM((FFL, TILE), BF), pltpu.VMEM((FFL, TILE), BF),
            pltpu.VMEM(rows, BF), pltpu.VMEM(rows, BF),
            pltpu.VMEM((4, 16, STEP), BF), pltpu.VMEM((8, 16, STEP), BF), pltpu.VMEM((XL, ROWS, TILE), F32),
            pltpu.VMEM((XL, 3, 2, QUART, FFL), F32), pltpu.VMEM((XL, 3, 2, QUART, FFL), F32), pltpu.VMEM((XL, 3, 2, QUART, FFL), F32),
            pltpu.VMEM((XL, 3, QUART, FFL), BF), pltpu.VMEM((XL, 3, QUART, FFL), BF),
            pltpu.VMEM((3, XL, 4, QUART, FFL), BF),
            pltpu.VMEM((2,) + rows, F32), pltpu.VMEM((2,) + rows, BF),
            pltpu.VMEM((2, XL, 2, 3, 4, ROWS, HALF), BF),
            pltpu.VMEM((2, XL, 2, 4, ROWS, HALF), F32), pltpu.VMEM((2, XL, 2, 4, ROWS, HALF), BF),
            pltpu.VMEM((2, XL, 2, 3, ROWS, HALF), BF),
            pltpu.VMEM((2, XL, ROWS, TILE), F32), pltpu.VMEM((ROWS, TILE), F32),
            pltpu.VMEM((8, 16, STEP), F32), pltpu.VMEM((4, 4 * TILE), F32),
            pltpu.VMEM((XL, 4, 16, STEP), BF), pltpu.VMEM((8, 16, STEP), BF),
            sem((3,)), sem((5,)), sem((7,)), sem((7,)), sem, sem,
            sem((2, XL, 2, 3)), sem((2, XL, 2, 3)), sem((2, XL, 2, 6)), sem((2, XL, 2, 6)),
            sem((XL, 2)), sem((XL, 2)), sem((XL, 2)), sem((XL, 2)), sem((XL, 2, 3)), sem((XL, 2, 3)),
            sem((2, XL, 2, 3)), sem((2, XL, 2, 3)), sem((2, XL, 2, 3)), sem((2, XL, 2, 3)),
            sem, sem, sem((XL, 4)), sem((XL, 4)),
        ],
        compiler_params=pltpu.CompilerParams(
            collective_id=0, has_side_effects=True, vmem_limit_bytes=62 * 1024 * 1024
        ),
        cost_estimate=pl.CostEstimate(flops=flops, bytes_accessed=20 * 1024 * 1024, transcendentals=0),
    )(act, cot, gate_proj, up_proj, down_proj)


def contract_rows(left, right):
    return lax.dot_general(left, right, (((0,), (0,)), ((), ())), preferred_element_type=F32).astype(BF)


def local(activations, cotangent, gate_proj, up_proj, down_proj):
    block_output, input_gradient, features, upstream, hid, gate_delta, up_delta = forward_backward(
        activations, cotangent, gate_proj.T, up_proj.T, down_proj
    )
    tokens = XL * Z * Y * ROWS
    features, upstream = features.reshape(tokens, TILE), upstream.reshape(tokens, TILE)
    hid, gate_delta, up_delta = (a.reshape(tokens, FFL) for a in (hid, gate_delta, up_delta))
    return (
        block_output,
        input_gradient,
        contract_rows(gate_delta, features).T,
        contract_rows(up_delta, features).T,
        contract_rows(hid, upstream),
    )


def solution(mesh):
    placed = (
        P(("wide", "narrow"), None),
        P("wide", "narrow"),
        P("narrow", "wide"),
        P("narrow", "wide"),
        P("wide", "narrow"),
    )
    return jax.shard_map(
        local,
        mesh=mesh,
        in_specs=placed,
        out_specs=(
            P("wide", "narrow"),
            P(("wide", "narrow"), None),
            P("narrow", "wide"),
            P("narrow", "wide"),
            P("wide", "narrow"),
        ),
        check_vma=False,
    )
```

```python
import jax
import jax.numpy as jnp
from jax import lax
from jax.experimental import pallas as pl
from jax.experimental.pallas import tpu as pltpu
from jax.sharding import PartitionSpec as P

MESH = pl.DeviceIdType.MESH
BF = jnp.bfloat16
F32 = jnp.float32

XL, Z, Y = 2, 4, 4
ROWS = 16
TILE = 2048
HALF = TILE // 2
FFL = 832
CHUNK = Z * Y * ROWS
PART = FFL // 2
STEP = 512


def dot(a, b):
    return lax.dot_general(a, b, (((1,), (0,)), ((), ())), preferred_element_type=F32)


def dot_t(a, b):
    return lax.dot_general(a, b, (((1,), (1,)), ((), ())), preferred_element_type=F32)


def kernel(
    act, cot, wg_hbm, wu_hbm, wd_hbm,
    out_ref, ig_ref, down_hbm, gate_hbm, up_hbm,
    wg, wu, wd, feat, cota, a_send, a_recv, a_f32,
    g_send, g_own, g_recv, x_send, x_recv, hd, ht,
    part, r1_send, r1_recv, s1, r2_send, r2_recv, xo_send, xo_recv, t_f32, o_f32, n_send, n_recv, grad,
    w_sem, o_sem, a_ss, a_rs, cx_ss, cx_rs, p1_ss, p1_rs, p2_ss, p2_rs,
    g_ss, g_rs, x_ss, x_rs, h_ss, h_rs, r1_ss, r1_rs, r2_ss, r2_rs, xo_ss, xo_rs, n_ss, n_rs,
):
    w = lax.axis_index("wide")
    n = lax.axis_index("narrow")
    y = lax.rem(w, Y)
    z = lax.rem(w // Y, Z)
    xl = w // (Y * Z)
    xh = n // 2
    core = lax.rem(n, 2)

    def wide_id(a, b, c):
        return (a * Z + b) * Y + c

    def y_dev(d):
        return (wide_id(xl, z, lax.rem(y + d, Y)), n)

    def z_dev(d):
        return (wide_id(xl, lax.rem(z + d, Z), y), n)

    def line_dev(dx, dn):
        return (wide_id(lax.rem(xl + dx, XL), z, y), lax.rem(n + dn, 4))

    sibling = (w, xh * 2 + (1 - core))
    across = (w, (1 - xh) * 2 + core)
    peer = (wide_id(1 - xl, z, y), n)
    line = [(dx, dn) for dx in range(XL) for dn in range(4) if (dx, dn) != (0, 0)]

    sends = []

    def remote(src, dst, ss, rs, dev):
        return pltpu.make_async_remote_copy(
            src_ref=src, dst_ref=dst, send_sem=ss, recv_sem=rs, device_id=dev, device_id_type=MESH
        )

    def send(src, dst, ss, rs, dev):
        copy = remote(src, dst, ss, rs, dev)
        copy.start()
        sends.append(copy)

    def landed(dst, ss, rs, dev):
        remote(dst, dst, ss, rs, dev).wait_recv()

    loads = [
        pltpu.make_async_copy(src, dst, w_sem.at[i])
        for i, (src, dst) in enumerate(((wg_hbm, wg), (wu_hbm, wu), (wd_hbm, wd)))
    ]
    for load in loads:
        load.start()

    barrier = pltpu.get_barrier_semaphore()
    friends = [y_dev(d) for d in (1, 2, 3)] + [z_dev(d) for d in (1, 2, 3)] + [line_dev(*k) for k in line]
    for dev in friends:
        pl.semaphore_signal(barrier, inc=1, device_id=dev, device_id_type=MESH)

    rows4 = act[...].astype(F32)
    for m in range(4):
        for k in range(4):
            at = m * TILE + k * STEP
            t_f32[m, pl.ds(4 * k, 4), :] = rows4[:, at : at + STEP]
    for m in range(4):
        a_send[m] = t_f32[m].astype(BF)
    cota[0, z, y] = cot[...]

    pl.semaphore_wait(barrier, len(friends))

    def exchange(dx):
        for i, (ex, dn) in enumerate(line):
            if ex == dx:
                send(a_send.at[lax.rem(n + dn, 4)], a_recv.at[4 * dx + n], a_ss.at[i], a_rs.at[i], line_dev(dx, dn))

    def assemble(dx):
        for i, (ex, dn) in enumerate(line):
            if ex == dx:
                landed(a_recv.at[4 * dx + lax.rem(n + 4 - dn, 4)], a_ss.at[i], a_rs.at[i], line_dev(dx, dn))
        for m in range(4):
            t_f32[m] = a_recv[4 * dx + m].astype(F32)
            for k in range(4):
                a_f32[dx, pl.ds(4 * m, 4), pl.ds(k * STEP, STEP)] = t_f32[m, pl.ds(4 * k, 4), :]
        feat[dx, z, y] = a_f32[dx].astype(BF)

    bufs = (feat, cota)
    cols = (pl.ds(0, HALF), pl.ds(HALF, HALF))

    def gather1(b, c):
        block = [bufs[b].at[c, z, y, :, cols[h]] for h in (0, 1)]
        for d in (1, 2, 3):
            send(block[0], block[0], p1_ss.at[b, c, 0, d - 1], p1_rs.at[b, c, 0, d - 1], z_dev(d))
            send(block[1], block[1], p1_ss.at[b, c, 1, d - 1], p1_rs.at[b, c, 1, d - 1], y_dev(d))

    def gather1_wait(b, c):
        for d in (1, 2, 3):
            landed(bufs[b].at[c, lax.rem(z + 4 - d, Z), y, :, cols[0]], p1_ss.at[b, c, 0, d - 1], p1_rs.at[b, c, 0, d - 1], z_dev(d))
            landed(bufs[b].at[c, z, lax.rem(y + 4 - d, Y), :, cols[1]], p1_ss.at[b, c, 1, d - 1], p1_rs.at[b, c, 1, d - 1], y_dev(d))

    low, high = pl.ds(0, 2), pl.ds(2, 2)

    def ring_block(b, c, h, back, part_of):
        if h == 0:
            return bufs[b].at[c, part_of, lax.rem(y + 4 - back, Y), :, cols[0]]
        return bufs[b].at[c, lax.rem(z + 4 - back, Z), part_of, :, cols[1]]

    def ring_dev(h, d):
        return y_dev(d) if h == 0 else z_dev(d)

    def gather2(b, c):
        for i, (d, part_of) in enumerate(((1, low), (3, high), (1, high), (3, low))):
            for h in (0, 1):
                block = ring_block(b, c, h, 0, part_of)
                send(block, block, p2_ss.at[b, c, h, i], p2_rs.at[b, c, h, i], ring_dev(h, d))

    def gather2_pass_on(b, c):
        for i, (d, part_of) in enumerate(((1, low), (3, high))):
            for h in (0, 1):
                block = ring_block(b, c, h, d, part_of)
                landed(block, p2_ss.at[b, c, h, i], p2_rs.at[b, c, h, i], ring_dev(h, d))
                send(block, block, p2_ss.at[b, c, h, 4 + i], p2_rs.at[b, c, h, 4 + i], ring_dev(h, d))

    def gather2_wait(b, c):
        for i, (d, back, part_of) in ((2, (1, 1, high)), (3, (3, 3, low)), (4, (1, 2, low)), (5, (3, 2, high))):
            for h in (0, 1):
                landed(ring_block(b, c, h, back, part_of), p2_ss.at[b, c, h, i], p2_rs.at[b, c, h, i], ring_dev(h, d))

    def partial(c, core_of, k, into):
        rows = pl.ds(pl.multiple_of(PART * core_of, PART), PART)
        into[c, k] = dot_t((wg, wu, wd)[k][rows, :], (feat, feat, cota)[k][c].reshape(CHUNK, TILE))

    def sum_send(c, k):
        partial(c, 1 - core, k, g_send)
        send(g_send.at[c, k], g_recv.at[c, k], g_ss.at[c, k], g_rs.at[c, k], sibling)

    def sum_own(c, k):
        partial(c, core, k, g_own)

    def sum_across(c, k):
        landed(g_recv.at[c, k], g_ss.at[c, k], g_rs.at[c, k], sibling)
        v = g_own[c, k] + g_recv[c, k]
        g_own[c, k] = v
        x_send[c, k] = v.astype(BF)
        send(x_send.at[c, k], x_recv.at[c, k], x_ss.at[c, k], x_rs.at[c, k], across)

    def arrived(c, k):
        landed(x_recv.at[c, k], x_ss.at[c, k], x_rs.at[c, k], across)
        return g_own[c, k] + x_recv[c, k].astype(F32)

    tokens = (pl.ds(0, CHUNK), pl.ds(CHUNK, CHUNK))

    def share(c, g):
        block = hd.at[pl.ds(*((0, 1), (1, 2))[g]), core, :, tokens[c]]
        send(block, block, h_ss.at[c, g], h_rs.at[c, g], sibling)

    def share_wait(c, g):
        block = hd.at[pl.ds(*((0, 1), (1, 2))[g]), 1 - core, :, tokens[c]]
        landed(block, h_ss.at[c, g], h_rs.at[c, g], sibling)

    def hidden(c):
        gate, up = arrived(c, 0), arrived(c, 1)
        g_own[c, 0] = gate
        g_own[c, 1] = up
        hd[0, core, :, tokens[c]] = (gate * lax.logistic(gate) * up).astype(BF)
        share(c, 0)

    def deltas(c):
        gate, up, back = g_own[c, 0], g_own[c, 1], arrived(c, 2)
        sigma = lax.logistic(gate)
        hd[1, core, :, tokens[c]] = (back * up * (sigma * (1.0 + gate * (1.0 - sigma)))).astype(BF)
        hd[2, core, :, tokens[c]] = (back * (gate * sigma)).astype(BF)
        share(c, 1)

    def product(k, c):
        for i in ((0,), (1, 2))[k]:
            ht[i] = hd[i, :, :, tokens[c]].reshape(FFL, CHUNK).T

        for h in (0, 1):
            if k == 0:
                v = dot(ht[0], wd[:, cols[h]])
            else:
                v = dot(ht[1], wg[:, cols[h]]) + dot(ht[2], wu[:, cols[h]])
            v = v.reshape(Z, Y, ROWS, HALF)
            part[...] = v
            r1_send[k, c, :, :, :, cols[h]] = v.astype(BF)
            for d in (1, 2, 3):
                to = lax.rem((y, z)[h] + d, 4)
                block = r1_send.at[k, c, :, to, :, cols[0]] if h == 0 else r1_send.at[k, c, to, :, :, cols[1]]
                send(block, r1_recv.at[k, c, h, d - 1], r1_ss.at[k, c, h, d - 1], r1_rs.at[k, c, h, d - 1], ring_dev(h, d))
            s1[k, c, h] = part[:, y] if h == 0 else part[z]

    def scatter2(k, c):
        for h in (0, 1):
            for d in (1, 2, 3):
                landed(r1_recv.at[k, c, h, d - 1], r1_ss.at[k, c, h, d - 1], r1_rs.at[k, c, h, d - 1], ring_dev(h, d))
            own = s1[k, c, h]
            for d in (1, 2, 3):
                own += r1_recv[k, c, h, d - 1].astype(F32)
            s1[k, c, h] = own
            r2_send[k, c, h] = own.astype(BF)
            for d in (1, 2, 3):
                to = lax.rem((z if h == 0 else y) + d, 4)
                send(r2_send.at[k, c, h, to], r2_recv.at[k, c, h, d - 1], r2_ss.at[k, c, h, d - 1], r2_rs.at[k, c, h, d - 1], ring_dev(1 - h, d))

    def scattered(k, c):
        for h in (0, 1):
            for d in (1, 2, 3):
                landed(r2_recv.at[k, c, h, d - 1], r2_ss.at[k, c, h, d - 1], r2_rs.at[k, c, h, d - 1], ring_dev(1 - h, d))
            own = s1[k, c, h, z if h == 0 else y]
            for d in (1, 2, 3):
                own += r2_recv[k, c, h, d - 1].astype(F32)
            xo_send[k, c, :, cols[h]] = own

    def owners(c):
        for m in range(4):
            for k in range(4):
                t_f32[m, pl.ds(4 * k, 4), :] = xo_send[1, c, pl.ds(4 * m, 4), pl.ds(k * STEP, STEP)]
        for m in range(4):
            n_send[c, m] = t_f32[m].astype(BF)
        for i, (dx, dn) in enumerate(line):
            if dx == c:
                send(n_send.at[c, lax.rem(n + dn, 4)], n_recv.at[4 * c + n], n_ss.at[i], n_rs.at[i], line_dev(dx, dn))

    stores = []

    def gradient(k):
        def columns(j, carry):
            at = pl.ds(pl.multiple_of(j * STEP, STEP), STEP)
            right = (cota, feat, feat)[k][:, :, :, :, at].reshape(XL * CHUNK, STEP)
            grad[k, :, at] = dot(hd[k].reshape(FFL, XL * CHUNK), right).astype(BF)
            return carry

        lax.fori_loop(0, TILE // STEP, columns, 0)
        stores.append(pltpu.make_async_copy(grad.at[k], (down_hbm, gate_hbm, up_hbm)[k], o_sem.at[k]))
        stores[-1].start()

    exchange(0)
    gather1(1, 0)
    exchange(1)
    send(cota.at[0, z, y], cota.at[1, z, y], cx_ss, cx_rs, peer)
    a_recv[n] = a_send[n]
    assemble(0)
    gather1(0, 0)
    gather1_wait(1, 0)
    gather2(1, 0)
    gather1_wait(0, 0)
    gather2(0, 0)
    gather2_pass_on(1, 0)
    assemble(1)
    gather1(0, 1)
    landed(cota.at[1, z, y], cx_ss, cx_rs, peer)
    gather1(1, 1)
    gather2_pass_on(0, 0)
    for load in loads:
        load.wait()
    gather1_wait(0, 1)
    gather2(0, 1)
    gather2_wait(0, 0)
    sum_send(0, 0)
    sum_send(0, 1)
    sum_own(0, 0)
    gather2_wait(1, 0)
    gather2_pass_on(0, 1)
    gather1_wait(1, 1)
    gather2(1, 1)
    sum_across(0, 0)
    sum_own(0, 1)
    sum_across(0, 1)
    sum_send(0, 2)
    sum_own(0, 2)
    sum_across(0, 2)
    gather2_wait(0, 1)
    sum_send(1, 0)
    sum_send(1, 1)
    gather2_pass_on(1, 1)
    sum_own(1, 0)
    sum_across(1, 0)
    sum_own(1, 1)
    sum_across(1, 1)
    hidden(0)
    gather2_wait(1, 1)
    sum_send(1, 2)
    share_wait(0, 0)
    product(0, 0)
    sum_own(1, 2)
    sum_across(1, 2)
    deltas(0)
    share_wait(0, 1)
    product(1, 0)
    scatter2(0, 0)
    hidden(1)
    share_wait(1, 0)
    product(0, 1)
    deltas(1)
    share_wait(1, 1)
    product(1, 1)
    scatter2(1, 0)
    gradient(0)
    scattered(0, 0)
    scatter2(0, 1)
    gradient(1)
    scattered(1, 0)
    owners(0)
    gradient(2)
    scattered(0, 1)
    send(xo_send.at[0, 1], xo_recv, xo_ss, xo_rs, peer)
    scatter2(1, 1)
    scattered(1, 1)
    owners(1)
    landed(xo_recv, xo_ss, xo_rs, peer)
    out_ref[...] = (xo_send[0, 0] + xo_recv[...]).astype(BF)
    n_recv[n] = n_send[0, n]
    for i, (dx, dn) in enumerate(line):
        landed(n_recv.at[4 * dx + lax.rem(n + 4 - dn, 4)], n_ss.at[i], n_rs.at[i], line_dev(dx, dn))
    for m in range(4):
        t_f32[m] = n_recv[m].astype(F32) + n_recv[4 + m].astype(F32)
        for k in range(4):
            at = m * TILE + k * STEP
            o_f32[:, pl.ds(at, STEP)] = t_f32[m, pl.ds(4 * k, 4), :]
    ig_ref[...] = o_f32[...].astype(BF)

    for copy in sends:
        copy.wait_send()
    for store in stores:
        store.wait()


def forward_backward(act, cot, gate_proj, up_proj, down_proj):
    any_space = pl.BlockSpec(memory_space=pl.ANY)
    vmem = pl.BlockSpec(memory_space=pltpu.VMEM)
    sem = pltpu.SemaphoreType.DMA
    rows = (XL, Z, Y, ROWS, TILE)
    like = jax.ShapeDtypeStruct
    flops = 2 * 9 * XL * Z * Y * ROWS * TILE * FFL
    return pl.pallas_call(
        kernel,
        name="ffn",
        out_shape=[
            like((ROWS, TILE), BF), like((4, 4 * TILE), BF),
            like((FFL, TILE), BF), like((FFL, TILE), BF), like((FFL, TILE), BF),
        ],
        in_specs=[vmem, vmem, any_space, any_space, any_space],
        out_specs=[vmem, vmem] + [any_space] * 3,
        scratch_shapes=[
            pltpu.VMEM((FFL, TILE), BF), pltpu.VMEM((FFL, TILE), BF), pltpu.VMEM((FFL, TILE), BF),
            pltpu.VMEM(rows, BF), pltpu.VMEM(rows, BF),
            pltpu.VMEM((4, 16, STEP), BF), pltpu.VMEM((8, 16, STEP), BF), pltpu.VMEM((XL, ROWS, TILE), F32),
            pltpu.VMEM((XL, 3, PART, CHUNK), F32), pltpu.VMEM((XL, 3, PART, CHUNK), F32), pltpu.VMEM((XL, 3, PART, CHUNK), F32),
            pltpu.VMEM((XL, 3, PART, CHUNK), BF), pltpu.VMEM((XL, 3, PART, CHUNK), BF),
            pltpu.VMEM((3, 2, PART, XL * CHUNK), BF), pltpu.VMEM((3, CHUNK, FFL), BF),
            pltpu.VMEM((Z, Y, ROWS, HALF), F32), pltpu.VMEM((2,) + rows, BF),
            pltpu.VMEM((2, XL, 2, 3, 4, ROWS, HALF), BF),
            pltpu.VMEM((2, XL, 2, 4, ROWS, HALF), F32), pltpu.VMEM((2, XL, 2, 4, ROWS, HALF), BF),
            pltpu.VMEM((2, XL, 2, 3, ROWS, HALF), BF),
            pltpu.VMEM((2, XL, ROWS, TILE), F32), pltpu.VMEM((ROWS, TILE), F32),
            pltpu.VMEM((8, 16, STEP), F32), pltpu.VMEM((4, 4 * TILE), F32),
            pltpu.VMEM((XL, 4, 16, STEP), BF), pltpu.VMEM((8, 16, STEP), BF), pltpu.VMEM((3, FFL, TILE), BF),
            sem((3,)), sem((3,)), sem((7,)), sem((7,)), sem, sem,
            sem((2, XL, 2, 3)), sem((2, XL, 2, 3)), sem((2, XL, 2, 6)), sem((2, XL, 2, 6)),
            sem((XL, 3)), sem((XL, 3)), sem((XL, 3)), sem((XL, 3)), sem((XL, 2)), sem((XL, 2)),
            sem((2, XL, 2, 3)), sem((2, XL, 2, 3)), sem((2, XL, 2, 3)), sem((2, XL, 2, 3)),
            sem, sem, sem((7,)), sem((7,)),
        ],
        compiler_params=pltpu.CompilerParams(
            collective_id=0, has_side_effects=True, vmem_limit_bytes=62 * 1024 * 1024
        ),
        cost_estimate=pl.CostEstimate(flops=flops, bytes_accessed=20 * 1024 * 1024, transcendentals=0),
    )(act, cot, gate_proj, up_proj, down_proj)


SLABS = 4


def move(*refs):
    srcs, dsts, held, sem_in, sem_out = refs[:5], refs[5:10], refs[10:15], refs[15], refs[16]
    parts = []
    for src, via, dst in zip(srcs, held, dsts):
        slabs = SLABS if src.shape[0] == FFL else 1
        rows = src.shape[0] // slabs
        for i in range(slabs):
            at, j = pl.ds(i * rows, rows), len(parts)
            parts.append((
                pltpu.make_async_copy(src.at[at], via.at[at], sem_in.at[j]),
                pltpu.make_async_copy(via.at[at], dst.at[at], sem_out.at[j]),
            ))
    for load, _ in parts:
        load.start()
    for load, store in parts:
        load.wait()
        store.start()
    for _, store in parts:
        store.wait()


def local(activations, cotangent, gate_proj, up_proj, down_proj):
    results = forward_backward(activations, cotangent, gate_proj.T, up_proj.T, down_proj)
    any_space = pl.BlockSpec(memory_space=pl.ANY)
    block_output, input_gradient, down_gradient, gate_gradient, up_gradient = pl.pallas_call(
        move,
        name="move",
        out_shape=[jax.ShapeDtypeStruct(r.shape, r.dtype) for r in results],
        in_specs=[any_space] * 5,
        out_specs=[any_space] * 5,
        scratch_shapes=[pltpu.VMEM(r.shape, r.dtype) for r in results]
        + [pltpu.SemaphoreType.DMA((3 * SLABS + 2,))] * 2,
        compiler_params=pltpu.CompilerParams(vmem_limit_bytes=62 * 1024 * 1024),
    )(*results)
    return block_output, input_gradient, gate_gradient.T, up_gradient.T, down_gradient


def solution(mesh):
    placed = (
        P(("wide", "narrow"), None),
        P("wide", "narrow"),
        P("narrow", "wide"),
        P("narrow", "wide"),
        P("wide", "narrow"),
    )
    return jax.shard_map(
        local,
        mesh=mesh,
        in_specs=placed,
        out_specs=(
            P("wide", "narrow"),
            P(("wide", "narrow"), None),
            P("narrow", "wide"),
            P("narrow", "wide"),
            P("wide", "narrow"),
        ),
        check_vma=False,
    )
```

```python
import jax
import jax.numpy as jnp
from jax import lax
from jax.experimental import pallas as pl
from jax.experimental.pallas import tpu as pltpu
from jax.sharding import PartitionSpec as P

MESH = pl.DeviceIdType.MESH
BF = jnp.bfloat16
F32 = jnp.float32

XL, Z, Y = 2, 4, 4
ROWS = 16
TILE = 2048
HALF = TILE // 2
FFL = 832
CHUNK = Z * Y * ROWS
SUB = CHUNK // 2
OWN = Z - 1
PART = FFL // 2
STEP = 512


def dot(a, b):
    return lax.dot_general(a, b, (((1,), (0,)), ((), ())), preferred_element_type=F32)


def dot_t(a, b):
    return lax.dot_general(a, b, (((1,), (1,)), ((), ())), preferred_element_type=F32)


def kernel(
    act, cot, wg_hbm, wu_hbm, wd_hbm,
    out_ref, ig_ref, down_hbm, gate_hbm, up_hbm,
    wg, wu, wd, feat, cota, a_send, a_recv, a_f32,
    g_send, g_own, g_recv, x_send, x_recv, hd, ht,
    part, r1_send, r1_recv, s1, r2_send, r2_recv, xo_send, xo_recv, t_f32, o_f32, n_send, n_recv, grad,
    w_sem, o_sem, a_ss, a_rs, cx_ss, cx_rs, p1_ss, p1_rs, p2_ss, p2_rs,
    g_ss, g_rs, x_ss, x_rs, h_ss, h_rs, r1_ss, r1_rs, r2_ss, r2_rs, xo_ss, xo_rs, n_ss, n_rs,
):
    w = lax.axis_index("wide")
    n = lax.axis_index("narrow")
    y = lax.rem(w, Y)
    z = lax.rem(w // Y, Z)
    xl = w // (Y * Z)
    xh = n // 2
    core = lax.rem(n, 2)

    def wide_id(a, b, c):
        return (a * Z + b) * Y + c

    def y_dev(d):
        return (wide_id(xl, z, lax.rem(y + d, Y)), n)

    def z_dev(d):
        return (wide_id(xl, lax.rem(z + d, Z), y), n)

    def line_dev(dx, dn):
        return (wide_id(lax.rem(xl + dx, XL), z, y), lax.rem(n + dn, 4))

    sibling = (w, xh * 2 + (1 - core))
    across = (w, (1 - xh) * 2 + core)
    peer = (wide_id(1 - xl, z, y), n)
    line = [(dx, dn) for dx in range(XL) for dn in range(4) if (dx, dn) != (0, 0)]

    sends = []

    def remote(src, dst, ss, rs, dev):
        return pltpu.make_async_remote_copy(
            src_ref=src, dst_ref=dst, send_sem=ss, recv_sem=rs, device_id=dev, device_id_type=MESH
        )

    def send(src, dst, ss, rs, dev):
        copy = remote(src, dst, ss, rs, dev)
        copy.start()
        sends.append(copy)

    def landed(dst, ss, rs, dev):
        remote(dst, dst, ss, rs, dev).wait_recv()

    loads = [
        pltpu.make_async_copy(src, dst, w_sem.at[i])
        for i, (src, dst) in enumerate(((wg_hbm, wg), (wu_hbm, wu), (wd_hbm, wd)))
    ]
    for load in loads:
        load.start()

    barrier = pltpu.get_barrier_semaphore()
    friends = [y_dev(d) for d in (1, 2, 3)] + [z_dev(d) for d in (1, 2, 3)] + [line_dev(*k) for k in line]
    for dev in friends:
        pl.semaphore_signal(barrier, inc=1, device_id=dev, device_id_type=MESH)

    rows4 = act[...].astype(F32)
    for m in range(4):
        for k in range(4):
            at = m * TILE + k * STEP
            t_f32[m, pl.ds(4 * k, 4), :] = rows4[:, at : at + STEP]
    for m in range(4):
        a_send[m] = t_f32[m].astype(BF)
    cota[0, OWN, y] = cot[...]

    pl.semaphore_wait(barrier, len(friends))

    def exchange(dx):
        for i, (ex, dn) in enumerate(line):
            if ex == dx:
                send(a_send.at[lax.rem(n + dn, 4)], a_recv.at[4 * dx + n], a_ss.at[i], a_rs.at[i], line_dev(dx, dn))

    def assemble(dx):
        for i, (ex, dn) in enumerate(line):
            if ex == dx:
                landed(a_recv.at[4 * dx + lax.rem(n + 4 - dn, 4)], a_ss.at[i], a_rs.at[i], line_dev(dx, dn))
        for m in range(4):
            t_f32[m] = a_recv[4 * dx + m].astype(F32)
            for k in range(4):
                a_f32[dx, pl.ds(4 * m, 4), pl.ds(k * STEP, STEP)] = t_f32[m, pl.ds(4 * k, 4), :]
        feat[dx, OWN, y] = a_f32[dx].astype(BF)

    bufs = (feat, cota)
    cols = (pl.ds(0, HALF), pl.ds(HALF, HALF))

    def gather1(b, c):
        block = [bufs[b].at[c, OWN, y, :, cols[h]] for h in (0, 1)]
        for d in (1, 2, 3):
            send(block[0], bufs[b].at[c, OWN - d, y, :, cols[0]], p1_ss.at[b, c, 0, d - 1], p1_rs.at[b, c, 0, d - 1], z_dev(d))
            send(block[1], block[1], p1_ss.at[b, c, 1, d - 1], p1_rs.at[b, c, 1, d - 1], y_dev(d))

    def gather1_wait(b, c):
        for d in (1, 2, 3):
            landed(bufs[b].at[c, OWN - d, y, :, cols[0]], p1_ss.at[b, c, 0, d - 1], p1_rs.at[b, c, 0, d - 1], z_dev(d))
            landed(bufs[b].at[c, OWN, lax.rem(y + 4 - d, Y), :, cols[1]], p1_ss.at[b, c, 1, d - 1], p1_rs.at[b, c, 1, d - 1], y_dev(d))

    low, high = pl.ds(0, 2), pl.ds(2, 2)

    def ring_block(b, c, h, back, part_of):
        if h == 0:
            return bufs[b].at[c, part_of, lax.rem(y + 4 - back, Y), :, cols[0]]
        return bufs[b].at[c, OWN - back, part_of, :, cols[1]]

    def ring_block_at(b, c, h, back, part_of, d):
        return ring_block(b, c, h, back if h == 0 else (back + d) % 4, part_of)

    def ring_dev(h, d):
        return y_dev(d) if h == 0 else z_dev(d)

    def gather2(b, c):
        for i, (d, part_of) in enumerate(((1, low), (3, high), (1, high), (3, low))):
            for h in (0, 1):
                block, there = ring_block(b, c, h, 0, part_of), ring_block_at(b, c, h, 0, part_of, d)
                send(block, there, p2_ss.at[b, c, h, i], p2_rs.at[b, c, h, i], ring_dev(h, d))

    def gather2_pass_on(b, c):
        for i, (d, part_of) in enumerate(((1, low), (3, high))):
            for h in (0, 1):
                block, there = ring_block(b, c, h, d, part_of), ring_block_at(b, c, h, d, part_of, d)
                landed(block, p2_ss.at[b, c, h, i], p2_rs.at[b, c, h, i], ring_dev(h, d))
                send(block, there, p2_ss.at[b, c, h, 4 + i], p2_rs.at[b, c, h, 4 + i], ring_dev(h, d))

    def gather2_wait(b, c):
        for i, (d, back, part_of) in ((2, (1, 1, high)), (3, (3, 3, low)), (4, (1, 2, low)), (5, (3, 2, high))):
            for h in (0, 1):
                landed(ring_block(b, c, h, back, part_of), p2_ss.at[b, c, h, i], p2_rs.at[b, c, h, i], ring_dev(h, d))

    def partial(c, core_of, k, into):
        rows = pl.ds(pl.multiple_of(PART * core_of, PART), PART)
        into[c, k] = dot_t((wg, wu, wd)[k][rows, :], (feat, feat, cota)[k][c].reshape(CHUNK, TILE))

    def sum_send(c, k):
        partial(c, 1 - core, k, g_send)
        send(g_send.at[c, k], g_recv.at[c, k], g_ss.at[c, k], g_rs.at[c, k], sibling)

    def sum_own(c, k):
        partial(c, core, k, g_own)

    subs = (pl.ds(0, SUB), pl.ds(SUB, SUB))

    def sum_chip(c, k):
        landed(g_recv.at[c, k], g_ss.at[c, k], g_rs.at[c, k], sibling)
        v = g_own[c, k] + g_recv[c, k]
        g_own[c, k] = v
        for s in (0, 1):
            x_send[c, k, s] = v[:, s * SUB : (s + 1) * SUB].astype(BF)

    def sum_across(c, k, s):
        send(x_send.at[c, k, s], x_recv.at[c, k, s], x_ss.at[c, k, s], x_rs.at[c, k, s], across)

    def arrived(c, k, s):
        landed(x_recv.at[c, k, s], x_ss.at[c, k, s], x_rs.at[c, k, s], across)
        return g_own[c, k, :, subs[s]] + x_recv[c, k, s].astype(F32)

    def tokens(c, s):
        return pl.ds(c * CHUNK + s * SUB, SUB)

    def share(c, s, g):
        block = hd.at[pl.ds(*((0, 1), (1, 2))[g]), core, :, tokens(c, s)]
        send(block, block, h_ss.at[c, s, g], h_rs.at[c, s, g], sibling)

    def share_wait(c, s, g):
        block = hd.at[pl.ds(*((0, 1), (1, 2))[g]), 1 - core, :, tokens(c, s)]
        landed(block, h_ss.at[c, s, g], h_rs.at[c, s, g], sibling)

    def hidden(c, s):
        gate, up = arrived(c, 0, s), arrived(c, 1, s)
        g_own[c, 0, :, subs[s]] = gate
        g_own[c, 1, :, subs[s]] = up
        hd[0, core, :, tokens(c, s)] = (gate * lax.logistic(gate) * up).astype(BF)
        share(c, s, 0)

    def deltas(c, s):
        gate, up, back = g_own[c, 0, :, subs[s]], g_own[c, 1, :, subs[s]], arrived(c, 2, s)
        sigma = lax.logistic(gate)
        hd[1, core, :, tokens(c, s)] = (back * up * (sigma * (1.0 + gate * (1.0 - sigma)))).astype(BF)
        hd[2, core, :, tokens(c, s)] = (back * (gate * sigma)).astype(BF)
        share(c, s, 1)

    def product(k, c, s):
        share_wait(c, s, k)
        for i in ((0,), (1, 2))[k]:
            ht[i] = hd[i, :, :, tokens(c, s)].reshape(FFL, SUB).T
        zs = pl.ds(2 * s, 2)
        for h in (0, 1):
            if k == 0:
                v = dot(ht[0], wd[:, cols[h]])
            else:
                v = dot(ht[1], wg[:, cols[h]]) + dot(ht[2], wu[:, cols[h]])
            v = v.reshape(2, Y, ROWS, HALF)
            part[...] = v
            r1_send[k, c, zs, :, :, cols[h]] = v.astype(BF)
            if h == 0:
                for d in (1, 2, 3):
                    send(r1_send.at[k, c, zs, lax.rem(y + d, Y), :, cols[0]], r1_recv.at[k, c, 0, d - 1, zs], r1_ss.at[k, c, s, d - 1], r1_rs.at[k, c, s, d - 1], y_dev(d))
                s1[k, c, 0, zs] = part[:, y]
            else:
                for j in (2 * s, 2 * s + 1):
                    if j == OWN:
                        s1[k, c, 1] = part[1]
                    else:
                        send(r1_send.at[k, c, j, :, :, cols[1]], r1_recv.at[k, c, 1, j], r1_ss.at[k, c, 2, j], r1_rs.at[k, c, 2, j], z_dev(j + 1))

    def scatter_z(k, c, s):
        zs = pl.ds(2 * s, 2)
        own = s1[k, c, 0, zs]
        for d in (1, 2, 3):
            landed(r1_recv.at[k, c, 0, d - 1, zs], r1_ss.at[k, c, s, d - 1], r1_rs.at[k, c, s, d - 1], y_dev(d))
            own += r1_recv[k, c, 0, d - 1, zs].astype(F32)
        s1[k, c, 0, zs] = own
        r2_send[k, c, 0, zs] = own.astype(BF)
        for j in (2 * s, 2 * s + 1):
            if j != OWN:
                send(r2_send.at[k, c, 0, j], r2_recv.at[k, c, 0, j], r2_ss.at[k, c, 0, j], r2_rs.at[k, c, 0, j], z_dev(j + 1))

    def scatter_y(k, c):
        own = s1[k, c, 1]
        for j in (0, 1, 2):
            landed(r1_recv.at[k, c, 1, j], r1_ss.at[k, c, 2, j], r1_rs.at[k, c, 2, j], z_dev(j + 1))
            own += r1_recv[k, c, 1, j].astype(F32)
        s1[k, c, 1] = own
        r2_send[k, c, 1] = own.astype(BF)
        for d in (1, 2, 3):
            send(r2_send.at[k, c, 1, lax.rem(y + d, Y)], r2_recv.at[k, c, 1, d - 1], r2_ss.at[k, c, 1, d - 1], r2_rs.at[k, c, 1, d - 1], y_dev(d))

    def scattered(k, c):
        for h in (0, 1):
            own = s1[k, c, h, OWN if h == 0 else y]
            for d in (1, 2, 3):
                landed(r2_recv.at[k, c, h, d - 1], r2_ss.at[k, c, h, d - 1], r2_rs.at[k, c, h, d - 1], ring_dev(1 - h, d))
                own += r2_recv[k, c, h, d - 1].astype(F32)
            xo_send[k, c, :, cols[h]] = own

    def owners(c):
        for m in range(4):
            for k in range(4):
                t_f32[m, pl.ds(4 * k, 4), :] = xo_send[1, c, pl.ds(4 * m, 4), pl.ds(k * STEP, STEP)]
        for m in range(4):
            n_send[c, m] = t_f32[m].astype(BF)
        for i, (dx, dn) in enumerate(line):
            if dx == c:
                send(n_send.at[c, lax.rem(n + dn, 4)], n_recv.at[4 * c + n], n_ss.at[i], n_rs.at[i], line_dev(dx, dn))

    stores = []

    def gradient(k):
        def columns(j, carry):
            at = pl.ds(pl.multiple_of(j * STEP, STEP), STEP)
            right = (cota, feat, feat)[k][:, :, :, :, at].reshape(XL * CHUNK, STEP)
            grad[k, :, at] = dot(hd[k].reshape(FFL, XL * CHUNK), right).astype(BF)
            return carry

        lax.fori_loop(0, TILE // STEP, columns, 0)
        stores.append(pltpu.make_async_copy(grad.at[k], (down_hbm, gate_hbm, up_hbm)[k], o_sem.at[k]))
        stores[-1].start()

    def sent(upto):
        for copy in sends[:upto]:
            copy.wait_send()
        del sends[:upto]

    exchange(0)
    gather1(1, 0)
    exchange(1)
    send(cota.at[0, OWN, y], cota.at[1, OWN, y], cx_ss, cx_rs, peer)
    a_recv[n] = a_send[n]
    assemble(0)
    gather1(0, 0)
    gather1_wait(1, 0)
    gather2(1, 0)
    gather1_wait(0, 0)
    gather2(0, 0)
    gather2_pass_on(1, 0)
    assemble(1)
    gather1(0, 1)
    landed(cota.at[1, OWN, y], cx_ss, cx_rs, peer)
    gather1(1, 1)
    gather2_pass_on(0, 0)
    for load in loads:
        load.wait()
    gather1_wait(0, 1)
    gather2(0, 1)
    gather2_wait(0, 0)
    sum_send(0, 0)
    sum_send(0, 1)
    sum_own(0, 0)
    gather2_wait(1, 0)
    gather2_pass_on(0, 1)
    gather1_wait(1, 1)
    gather2(1, 1)
    sum_chip(0, 0)
    sum_across(0, 0, 0)
    sum_own(0, 1)
    sum_chip(0, 1)
    sum_across(0, 1, 0)
    sum_across(0, 0, 1)
    sum_across(0, 1, 1)
    sum_send(0, 2)
    sum_own(0, 2)
    sum_chip(0, 2)
    sum_across(0, 2, 0)
    sum_across(0, 2, 1)
    gather2_wait(0, 1)
    sum_send(1, 0)
    sum_send(1, 1)
    gather2_pass_on(1, 1)
    hidden(0, 0)
    sum_own(1, 0)
    product(0, 0, 0)
    sum_chip(1, 0)
    sum_across(1, 0, 0)
    sum_own(1, 1)
    sum_chip(1, 1)
    sum_across(1, 1, 0)
    sum_across(1, 0, 1)
    sum_across(1, 1, 1)
    hidden(0, 1)
    gather2_wait(1, 1)
    sum_send(1, 2)
    product(0, 0, 1)
    deltas(0, 0)
    sum_own(1, 2)
    sum_chip(1, 2)
    sum_across(1, 2, 0)
    sum_across(1, 2, 1)
    product(1, 0, 0)
    deltas(0, 1)
    scatter_z(0, 0, 0)
    product(1, 0, 1)
    scatter_z(0, 0, 1)
    scatter_y(0, 0)
    hidden(1, 0)
    product(0, 1, 0)
    hidden(1, 1)
    scatter_z(1, 0, 0)
    product(0, 1, 1)
    scatter_z(1, 0, 1)
    scatter_y(1, 0)
    deltas(1, 0)
    product(1, 1, 0)
    early = len(sends)
    deltas(1, 1)
    product(1, 1, 1)
    scatter_z(0, 1, 0)
    scatter_z(0, 1, 1)
    scatter_y(0, 1)
    scattered(0, 0)
    scattered(1, 0)
    owners(0)
    gradient(0)
    scatter_z(1, 1, 0)
    gradient(1)
    scatter_z(1, 1, 1)
    scatter_y(1, 1)
    scattered(0, 1)
    send(xo_send.at[0, 1], xo_recv, xo_ss, xo_rs, peer)
    gradient(2)
    sent(early)
    scattered(1, 1)
    owners(1)
    landed(xo_recv, xo_ss, xo_rs, peer)
    out_ref[...] = (xo_send[0, 0] + xo_recv[...]).astype(BF)
    n_recv[n] = n_send[0, n]
    for i, (dx, dn) in enumerate(line):
        landed(n_recv.at[4 * dx + lax.rem(n + 4 - dn, 4)], n_ss.at[i], n_rs.at[i], line_dev(dx, dn))
    for m in range(4):
        t_f32[m] = n_recv[m].astype(F32) + n_recv[4 + m].astype(F32)
        for k in range(4):
            at = m * TILE + k * STEP
            o_f32[:, pl.ds(at, STEP)] = t_f32[m, pl.ds(4 * k, 4), :]
    ig_ref[...] = o_f32[...].astype(BF)

    sent(len(sends))
    for store in stores:
        store.wait()


def forward_backward(act, cot, gate_proj, up_proj, down_proj):
    any_space = pl.BlockSpec(memory_space=pl.ANY)
    vmem = pl.BlockSpec(memory_space=pltpu.VMEM)
    sem = pltpu.SemaphoreType.DMA
    rows = (XL, Z, Y, ROWS, TILE)
    like = jax.ShapeDtypeStruct
    flops = 2 * 9 * XL * Z * Y * ROWS * TILE * FFL
    return pl.pallas_call(
        kernel,
        name="ffn",
        out_shape=[
            like((ROWS, TILE), BF), like((4, 4 * TILE), BF),
            like((FFL, TILE), BF), like((FFL, TILE), BF), like((FFL, TILE), BF),
        ],
        in_specs=[vmem, vmem, any_space, any_space, any_space],
        out_specs=[vmem, vmem] + [any_space] * 3,
        scratch_shapes=[
            pltpu.VMEM((FFL, TILE), BF), pltpu.VMEM((FFL, TILE), BF), pltpu.VMEM((FFL, TILE), BF),
            pltpu.VMEM(rows, BF), pltpu.VMEM(rows, BF),
            pltpu.VMEM((4, 16, STEP), BF), pltpu.VMEM((8, 16, STEP), BF), pltpu.VMEM((XL, ROWS, TILE), F32),
            pltpu.VMEM((XL, 3, PART, CHUNK), F32), pltpu.VMEM((XL, 3, PART, CHUNK), F32), pltpu.VMEM((XL, 3, PART, CHUNK), F32),
            pltpu.VMEM((XL, 3, 2, PART, SUB), BF), pltpu.VMEM((XL, 3, 2, PART, SUB), BF),
            pltpu.VMEM((3, 2, PART, XL * CHUNK), BF), pltpu.VMEM((3, SUB, FFL), BF),
            pltpu.VMEM((2, Y, ROWS, HALF), F32), pltpu.VMEM((2,) + rows, BF),
            pltpu.VMEM((2, XL, 2, 3, 4, ROWS, HALF), BF),
            pltpu.VMEM((2, XL, 2, 4, ROWS, HALF), F32), pltpu.VMEM((2, XL, 2, 4, ROWS, HALF), BF),
            pltpu.VMEM((2, XL, 2, 3, ROWS, HALF), BF),
            pltpu.VMEM((2, XL, ROWS, TILE), F32), pltpu.VMEM((ROWS, TILE), F32),
            pltpu.VMEM((8, 16, STEP), F32), pltpu.VMEM((4, 4 * TILE), F32),
            pltpu.VMEM((XL, 4, 16, STEP), BF), pltpu.VMEM((8, 16, STEP), BF), pltpu.VMEM((3, FFL, TILE), BF),
            sem((3,)), sem((3,)), sem((7,)), sem((7,)), sem, sem,
            sem((2, XL, 2, 3)), sem((2, XL, 2, 3)), sem((2, XL, 2, 6)), sem((2, XL, 2, 6)),
            sem((XL, 3)), sem((XL, 3)), sem((XL, 3, 2)), sem((XL, 3, 2)), sem((XL, 2, 2)), sem((XL, 2, 2)),
            sem((2, XL, 3, 3)), sem((2, XL, 3, 3)), sem((2, XL, 2, 3)), sem((2, XL, 2, 3)),
            sem, sem, sem((7,)), sem((7,)),
        ],
        compiler_params=pltpu.CompilerParams(
            collective_id=0, has_side_effects=True, vmem_limit_bytes=62 * 1024 * 1024
        ),
        cost_estimate=pl.CostEstimate(flops=flops, bytes_accessed=20 * 1024 * 1024, transcendentals=0),
    )(act, cot, gate_proj, up_proj, down_proj)


SLABS = 4


def move(*refs):
    srcs, dsts, held, sem_in, sem_out = refs[:5], refs[5:10], refs[10:15], refs[15], refs[16]
    parts = []
    for src, via, dst in zip(srcs, held, dsts):
        slabs = SLABS if src.shape[0] == FFL else 1
        rows = src.shape[0] // slabs
        for i in range(slabs):
            at, j = pl.ds(i * rows, rows), len(parts)
            parts.append((
                pltpu.make_async_copy(src.at[at], via.at[at], sem_in.at[j]),
                pltpu.make_async_copy(via.at[at], dst.at[at], sem_out.at[j]),
            ))
    for load, _ in parts:
        load.start()
    for load, store in parts:
        load.wait()
        store.start()
    for _, store in parts:
        store.wait()


def local(activations, cotangent, gate_proj, up_proj, down_proj):
    results = forward_backward(activations, cotangent, gate_proj.T, up_proj.T, down_proj)
    any_space = pl.BlockSpec(memory_space=pl.ANY)
    block_output, input_gradient, down_gradient, gate_gradient, up_gradient = pl.pallas_call(
        move,
        name="move",
        out_shape=[jax.ShapeDtypeStruct(r.shape, r.dtype) for r in results],
        in_specs=[any_space] * 5,
        out_specs=[any_space] * 5,
        scratch_shapes=[pltpu.VMEM(r.shape, r.dtype) for r in results]
        + [pltpu.SemaphoreType.DMA((3 * SLABS + 2,))] * 2,
        compiler_params=pltpu.CompilerParams(vmem_limit_bytes=62 * 1024 * 1024),
    )(*results)
    return block_output, input_gradient, gate_gradient.T, up_gradient.T, down_gradient


def solution(mesh):
    placed = (
        P(("wide", "narrow"), None),
        P("wide", "narrow"),
        P("narrow", "wide"),
        P("narrow", "wide"),
        P("wide", "narrow"),
    )
    return jax.shard_map(
        local,
        mesh=mesh,
        in_specs=placed,
        out_specs=(
            P("wide", "narrow"),
            P(("wide", "narrow"), None),
            P("narrow", "wide"),
            P("narrow", "wide"),
            P("wide", "narrow"),
        ),
        check_vma=False,
    )
```

```python
import jax
import jax.numpy as jnp
from jax import lax
from jax.experimental import pallas as pl
from jax.experimental.pallas import tpu as pltpu
from jax.sharding import PartitionSpec as P

MESH = pl.DeviceIdType.MESH
BF = jnp.bfloat16
F32 = jnp.float32

XL, Z, Y = 2, 4, 4
ROWS = 16
TILE = 2048
HALF = TILE // 2
FFL = 832
CHUNK = Z * Y * ROWS
SUB = CHUNK // 2
OWN = Z - 1
PART = FFL // 2
STEP = 512


def dot(a, b):
    return lax.dot_general(a, b, (((1,), (0,)), ((), ())), preferred_element_type=F32)


def dot_t(a, b):
    return lax.dot_general(a, b, (((1,), (1,)), ((), ())), preferred_element_type=F32)


def kernel(
    act, cot, wg_hbm, wu_hbm, wd_hbm,
    out_ref, ig_ref, down_hbm, f_hbm, gd_hbm, ud_hbm,
    wg, wu, wd, feat, cota, a_send, a_recv, a_f32,
    g_send, g_own, g_recv, x_send, x_recv, hd, ht,
    part, r1_send, r1_recv, s1, r2_send, r2_recv, xo_send, xo_recv, t_f32, o_f32, n_send, n_recv, grad,
    w_sem, o_sem, a_ss, a_rs, cx_ss, cx_rs, p1_ss, p1_rs, p2_ss, p2_rs,
    g_ss, g_rs, x_ss, x_rs, h_ss, h_rs, r1_ss, r1_rs, r2_ss, r2_rs, xo_ss, xo_rs, n_ss, n_rs,
):
    w = lax.axis_index("wide")
    n = lax.axis_index("narrow")
    y = lax.rem(w, Y)
    z = lax.rem(w // Y, Z)
    xl = w // (Y * Z)
    xh = n // 2
    core = lax.rem(n, 2)

    def wide_id(a, b, c):
        return (a * Z + b) * Y + c

    def y_dev(d):
        return (wide_id(xl, z, lax.rem(y + d, Y)), n)

    def z_dev(d):
        return (wide_id(xl, lax.rem(z + d, Z), y), n)

    def line_dev(dx, dn):
        return (wide_id(lax.rem(xl + dx, XL), z, y), lax.rem(n + dn, 4))

    sibling = (w, xh * 2 + (1 - core))
    across = (w, (1 - xh) * 2 + core)
    peer = (wide_id(1 - xl, z, y), n)
    line = [(dx, dn) for dx in range(XL) for dn in range(4) if (dx, dn) != (0, 0)]

    sends = []

    def remote(src, dst, ss, rs, dev):
        return pltpu.make_async_remote_copy(
            src_ref=src, dst_ref=dst, send_sem=ss, recv_sem=rs, device_id=dev, device_id_type=MESH
        )

    def send(src, dst, ss, rs, dev):
        copy = remote(src, dst, ss, rs, dev)
        copy.start()
        sends.append(copy)

    def landed(dst, ss, rs, dev):
        remote(dst, dst, ss, rs, dev).wait_recv()

    loads = [
        pltpu.make_async_copy(src, dst, w_sem.at[i])
        for i, (src, dst) in enumerate(((wg_hbm, wg), (wu_hbm, wu), (wd_hbm, wd)))
    ]
    for load in loads:
        load.start()

    barrier = pltpu.get_barrier_semaphore()
    friends = [y_dev(d) for d in (1, 2, 3)] + [z_dev(d) for d in (1, 2, 3)] + [line_dev(*k) for k in line]
    for dev in friends:
        pl.semaphore_signal(barrier, inc=1, device_id=dev, device_id_type=MESH)

    rows4 = act[...].astype(F32)
    for m in range(4):
        for k in range(4):
            at = m * TILE + k * STEP
            t_f32[m, pl.ds(4 * k, 4), :] = rows4[:, at : at + STEP]
    for m in range(4):
        a_send[m] = t_f32[m].astype(BF)
    cota[0, OWN, y] = cot[...]

    pl.semaphore_wait(barrier, len(friends))

    def exchange(dx):
        for i, (ex, dn) in enumerate(line):
            if ex == dx:
                send(a_send.at[lax.rem(n + dn, 4)], a_recv.at[4 * dx + n], a_ss.at[i], a_rs.at[i], line_dev(dx, dn))

    def assemble(dx):
        for i, (ex, dn) in enumerate(line):
            if ex == dx:
                landed(a_recv.at[4 * dx + lax.rem(n + 4 - dn, 4)], a_ss.at[i], a_rs.at[i], line_dev(dx, dn))
        for m in range(4):
            t_f32[m] = a_recv[4 * dx + m].astype(F32)
            for k in range(4):
                a_f32[dx, pl.ds(4 * m, 4), pl.ds(k * STEP, STEP)] = t_f32[m, pl.ds(4 * k, 4), :]
        feat[dx, OWN, y] = a_f32[dx].astype(BF)

    bufs = (feat, cota)
    cols = (pl.ds(0, HALF), pl.ds(HALF, HALF))

    def gather1(b, c):
        block = [bufs[b].at[c, OWN, y, :, cols[h]] for h in (0, 1)]
        for d in (1, 2, 3):
            send(block[0], bufs[b].at[c, OWN - d, y, :, cols[0]], p1_ss.at[b, c, 0, d - 1], p1_rs.at[b, c, 0, d - 1], z_dev(d))
            send(block[1], block[1], p1_ss.at[b, c, 1, d - 1], p1_rs.at[b, c, 1, d - 1], y_dev(d))

    def gather1_wait(b, c):
        for d in (1, 2, 3):
            landed(bufs[b].at[c, OWN - d, y, :, cols[0]], p1_ss.at[b, c, 0, d - 1], p1_rs.at[b, c, 0, d - 1], z_dev(d))
            landed(bufs[b].at[c, OWN, lax.rem(y + 4 - d, Y), :, cols[1]], p1_ss.at[b, c, 1, d - 1], p1_rs.at[b, c, 1, d - 1], y_dev(d))

    low, high = pl.ds(0, 2), pl.ds(2, 2)

    def ring_block(b, c, h, back, part_of):
        if h == 0:
            return bufs[b].at[c, part_of, lax.rem(y + 4 - back, Y), :, cols[0]]
        return bufs[b].at[c, OWN - back, part_of, :, cols[1]]

    def ring_block_at(b, c, h, back, part_of, d):
        return ring_block(b, c, h, back if h == 0 else (back + d) % 4, part_of)

    def ring_dev(h, d):
        return y_dev(d) if h == 0 else z_dev(d)

    def gather2(b, c):
        for i, (d, part_of) in enumerate(((1, low), (3, high), (1, high), (3, low))):
            for h in (0, 1):
                block, there = ring_block(b, c, h, 0, part_of), ring_block_at(b, c, h, 0, part_of, d)
                send(block, there, p2_ss.at[b, c, h, i], p2_rs.at[b, c, h, i], ring_dev(h, d))

    def gather2_direct(b, c):
        for d in (1, 2, 3):
            for h in (0, 1):
                block, there = ring_block(b, c, h, 0, pl.ds(0, 4)), ring_block_at(b, c, h, 0, pl.ds(0, 4), d)
                send(block, there, p2_ss.at[b, c, h, d - 1], p2_rs.at[b, c, h, d - 1], ring_dev(h, d))

    def gather2_direct_wait(b, c):
        for d in (1, 2, 3):
            for h in (0, 1):
                landed(ring_block(b, c, h, d, pl.ds(0, 4)), p2_ss.at[b, c, h, d - 1], p2_rs.at[b, c, h, d - 1], ring_dev(h, d))

    def gather2_pass_on(b, c):
        for i, (d, part_of) in enumerate(((1, low), (3, high))):
            for h in (0, 1):
                block, there = ring_block(b, c, h, d, part_of), ring_block_at(b, c, h, d, part_of, d)
                landed(block, p2_ss.at[b, c, h, i], p2_rs.at[b, c, h, i], ring_dev(h, d))
                send(block, there, p2_ss.at[b, c, h, 4 + i], p2_rs.at[b, c, h, 4 + i], ring_dev(h, d))

    def gather2_wait(b, c):
        for i, (d, back, part_of) in ((2, (1, 1, high)), (3, (3, 3, low)), (4, (1, 2, low)), (5, (3, 2, high))):
            for h in (0, 1):
                landed(ring_block(b, c, h, back, part_of), p2_ss.at[b, c, h, i], p2_rs.at[b, c, h, i], ring_dev(h, d))

    def partial(c, core_of, k, into):
        rows = pl.ds(pl.multiple_of(PART * core_of, PART), PART)
        into[c, k] = dot_t((wg, wu, wd)[k][rows, :], (feat, feat, cota)[k][c].reshape(CHUNK, TILE))

    def sum_send(c, k):
        partial(c, 1 - core, k, g_send)
        send(g_send.at[c, k], g_recv.at[c, k], g_ss.at[c, k], g_rs.at[c, k], sibling)

    def sum_own(c, k):
        partial(c, core, k, g_own)

    subs = (pl.ds(0, SUB), pl.ds(SUB, SUB))

    def sum_chip(c, k):
        landed(g_recv.at[c, k], g_ss.at[c, k], g_rs.at[c, k], sibling)
        v = g_own[c, k] + g_recv[c, k]
        g_own[c, k] = v
        for s in (0, 1):
            x_send[c, k, s] = v[:, s * SUB : (s + 1) * SUB].astype(BF)

    def sum_across(c, k, s):
        send(x_send.at[c, k, s], x_recv.at[c, k, s], x_ss.at[c, k, s], x_rs.at[c, k, s], across)

    def arrived(c, k, s):
        landed(x_recv.at[c, k, s], x_ss.at[c, k, s], x_rs.at[c, k, s], across)
        return g_own[c, k, :, subs[s]] + x_recv[c, k, s].astype(F32)

    def tokens(c, s):
        return pl.ds(c * CHUNK + s * SUB, SUB)

    def share(c, s, g):
        block = hd.at[pl.ds(*((0, 1), (1, 2))[g]), core, :, tokens(c, s)]
        send(block, block, h_ss.at[c, s, g], h_rs.at[c, s, g], sibling)

    def share_wait(c, s, g):
        block = hd.at[pl.ds(*((0, 1), (1, 2))[g]), 1 - core, :, tokens(c, s)]
        landed(block, h_ss.at[c, s, g], h_rs.at[c, s, g], sibling)

    def hidden(c, s):
        gate, up = arrived(c, 0, s), arrived(c, 1, s)
        g_own[c, 0, :, subs[s]] = gate
        g_own[c, 1, :, subs[s]] = up
        hd[0, core, :, tokens(c, s)] = (gate * lax.logistic(gate) * up).astype(BF)
        share(c, s, 0)

    def deltas(c, s):
        gate, up, back = g_own[c, 0, :, subs[s]], g_own[c, 1, :, subs[s]], arrived(c, 2, s)
        sigma = lax.logistic(gate)
        hd[1, core, :, tokens(c, s)] = (back * up * (sigma * (1.0 + gate * (1.0 - sigma)))).astype(BF)
        hd[2, core, :, tokens(c, s)] = (back * (gate * sigma)).astype(BF)
        share(c, s, 1)

    def product(k, c, s):
        share_wait(c, s, k)
        for i in ((0,), (1, 2))[k]:
            ht[i] = hd[i, :, :, tokens(c, s)].reshape(FFL, SUB).T
        zs = pl.ds(2 * s, 2)
        for h in (0, 1):
            if k == 0:
                v = dot(ht[0], wd[:, cols[h]])
            else:
                v = dot(ht[1], wg[:, cols[h]]) + dot(ht[2], wu[:, cols[h]])
            v = v.reshape(2, Y, ROWS, HALF)
            part[...] = v
            r1_send[k, c, zs, :, :, cols[h]] = v.astype(BF)
            if h == 0:
                for d in (1, 2, 3):
                    send(r1_send.at[k, c, zs, lax.rem(y + d, Y), :, cols[0]], r1_recv.at[k, c, 0, d - 1, zs], r1_ss.at[k, c, s, d - 1], r1_rs.at[k, c, s, d - 1], y_dev(d))
                s1[k, c, 0, zs] = part[:, y]
            else:
                for j in (2 * s, 2 * s + 1):
                    if j == OWN:
                        s1[k, c, 1] = part[1]
                    else:
                        send(r1_send.at[k, c, j, :, :, cols[1]], r1_recv.at[k, c, 1, j], r1_ss.at[k, c, 2, j], r1_rs.at[k, c, 2, j], z_dev(j + 1))

    def scatter_z(k, c, s):
        zs = pl.ds(2 * s, 2)
        own = s1[k, c, 0, zs]
        for d in (1, 2, 3):
            landed(r1_recv.at[k, c, 0, d - 1, zs], r1_ss.at[k, c, s, d - 1], r1_rs.at[k, c, s, d - 1], y_dev(d))
            own += r1_recv[k, c, 0, d - 1, zs].astype(F32)
        s1[k, c, 0, zs] = own
        r2_send[k, c, 0, zs] = own.astype(BF)
        for j in (2 * s, 2 * s + 1):
            if j != OWN:
                send(r2_send.at[k, c, 0, j], r2_recv.at[k, c, 0, j], r2_ss.at[k, c, 0, j], r2_rs.at[k, c, 0, j], z_dev(j + 1))

    def scatter_y(k, c):
        own = s1[k, c, 1]
        for j in (0, 1, 2):
            landed(r1_recv.at[k, c, 1, j], r1_ss.at[k, c, 2, j], r1_rs.at[k, c, 2, j], z_dev(j + 1))
            own += r1_recv[k, c, 1, j].astype(F32)
        s1[k, c, 1] = own
        r2_send[k, c, 1] = own.astype(BF)
        for d in (1, 2, 3):
            send(r2_send.at[k, c, 1, lax.rem(y + d, Y)], r2_recv.at[k, c, 1, d - 1], r2_ss.at[k, c, 1, d - 1], r2_rs.at[k, c, 1, d - 1], y_dev(d))

    def scattered(k, c):
        for h in (0, 1):
            own = s1[k, c, h, OWN if h == 0 else y]
            for d in (1, 2, 3):
                landed(r2_recv.at[k, c, h, d - 1], r2_ss.at[k, c, h, d - 1], r2_rs.at[k, c, h, d - 1], ring_dev(1 - h, d))
                own += r2_recv[k, c, h, d - 1].astype(F32)
            xo_send[k, c, :, cols[h]] = own

    def owners(c):
        for m in range(4):
            for k in range(4):
                t_f32[m, pl.ds(4 * k, 4), :] = xo_send[1, c, pl.ds(4 * m, 4), pl.ds(k * STEP, STEP)]
        for m in range(4):
            n_send[c, m] = t_f32[m].astype(BF)
        for i, (dx, dn) in enumerate(line):
            if dx == c:
                send(n_send.at[c, lax.rem(n + dn, 4)], n_recv.at[4 * c + n], n_ss.at[i], n_rs.at[i], line_dev(dx, dn))

    stores = []

    def store(src, dst):
        stores.append(pltpu.make_async_copy(src, dst, o_sem.at[len(stores)]))
        stores[-1].start()

    def down_gradient():
        def columns(j, carry):
            at = pl.ds(pl.multiple_of(j * STEP, STEP), STEP)
            right = cota[:, :, :, :, at].reshape(XL * CHUNK, STEP)
            grad[:, at] = dot(hd[0].reshape(FFL, XL * CHUNK), right).astype(BF)
            return carry

        lax.fori_loop(0, TILE // STEP, columns, 0)
        store(grad, down_hbm)

    def sent(upto):
        for copy in sends[:upto]:
            copy.wait_send()
        del sends[:upto]

    exchange(0)
    gather1(1, 0)
    exchange(1)
    send(cota.at[0, OWN, y], cota.at[1, OWN, y], cx_ss, cx_rs, peer)
    a_recv[n] = a_send[n]
    assemble(0)
    gather1(0, 0)
    gather1_wait(0, 0)
    gather2_direct(0, 0)
    gather1_wait(1, 0)
    gather2(1, 0)
    assemble(1)
    gather1(0, 1)
    landed(cota.at[1, OWN, y], cx_ss, cx_rs, peer)
    gather1(1, 1)
    for load in loads:
        load.wait()
    gather2_direct_wait(0, 0)
    sum_send(0, 0)
    sum_send(0, 1)
    sum_own(0, 0)
    gather2_pass_on(1, 0)
    gather1_wait(0, 1)
    gather2(0, 1)
    sum_chip(0, 0)
    sum_across(0, 0, 0)
    sum_own(0, 1)
    sum_chip(0, 1)
    sum_across(0, 1, 0)
    sum_across(0, 0, 1)
    sum_across(0, 1, 1)
    gather2_wait(1, 0)
    sum_send(0, 2)
    gather2_pass_on(0, 1)
    gather1_wait(1, 1)
    gather2(1, 1)
    sum_own(0, 2)
    sum_chip(0, 2)
    sum_across(0, 2, 0)
    sum_across(0, 2, 1)
    gather2_wait(0, 1)
    sum_send(1, 0)
    sum_send(1, 1)
    gather2_pass_on(1, 1)
    hidden(0, 0)
    sum_own(1, 0)
    product(0, 0, 0)
    sum_chip(1, 0)
    sum_across(1, 0, 0)
    sum_own(1, 1)
    sum_chip(1, 1)
    sum_across(1, 1, 0)
    sum_across(1, 0, 1)
    sum_across(1, 1, 1)
    hidden(0, 1)
    gather2_wait(1, 1)
    sum_send(1, 2)
    product(0, 0, 1)
    deltas(0, 0)
    sum_own(1, 2)
    sum_chip(1, 2)
    sum_across(1, 2, 0)
    sum_across(1, 2, 1)
    product(1, 0, 0)
    deltas(0, 1)
    scatter_z(0, 0, 0)
    product(1, 0, 1)
    scatter_z(0, 0, 1)
    scatter_y(0, 0)
    hidden(1, 0)
    product(0, 1, 0)
    hidden(1, 1)
    scatter_z(1, 0, 0)
    product(0, 1, 1)
    scatter_z(1, 0, 1)
    scatter_y(1, 0)
    deltas(1, 0)
    product(1, 1, 0)
    early = len(sends)
    deltas(1, 1)
    product(1, 1, 1)
    store(feat, f_hbm)
    store(hd.at[1], gd_hbm)
    store(hd.at[2], ud_hbm)
    scatter_z(0, 1, 0)
    scatter_z(0, 1, 1)
    scatter_y(0, 1)
    scattered(0, 0)
    scattered(1, 0)
    owners(0)
    down_gradient()
    scatter_z(1, 1, 0)
    scatter_z(1, 1, 1)
    scatter_y(1, 1)
    scattered(0, 1)
    send(xo_send.at[0, 1], xo_recv, xo_ss, xo_rs, peer)
    sent(early)
    scattered(1, 1)
    owners(1)
    landed(xo_recv, xo_ss, xo_rs, peer)
    out_ref[...] = (xo_send[0, 0] + xo_recv[...]).astype(BF)
    n_recv[n] = n_send[0, n]
    for i, (dx, dn) in enumerate(line):
        landed(n_recv.at[4 * dx + lax.rem(n + 4 - dn, 4)], n_ss.at[i], n_rs.at[i], line_dev(dx, dn))
    for m in range(4):
        t_f32[m] = n_recv[m].astype(F32) + n_recv[4 + m].astype(F32)
        for k in range(4):
            at = m * TILE + k * STEP
            o_f32[:, pl.ds(at, STEP)] = t_f32[m, pl.ds(4 * k, 4), :]
    ig_ref[...] = o_f32[...].astype(BF)

    sent(len(sends))
    for copy in stores:
        copy.wait()


def forward_backward(act, cot, gate_proj, up_proj, down_proj):
    any_space = pl.BlockSpec(memory_space=pl.ANY)
    vmem = pl.BlockSpec(memory_space=pltpu.VMEM)
    sem = pltpu.SemaphoreType.DMA
    rows = (XL, Z, Y, ROWS, TILE)
    like = jax.ShapeDtypeStruct
    flops = 2 * 7 * XL * Z * Y * ROWS * TILE * FFL
    return pl.pallas_call(
        kernel,
        name="ffn",
        out_shape=[
            like((ROWS, TILE), BF), like((4, 4 * TILE), BF),
            like((FFL, TILE), BF), like(rows, BF), like((2, PART, XL * CHUNK), BF), like((2, PART, XL * CHUNK), BF),
        ],
        in_specs=[vmem, vmem, any_space, any_space, any_space],
        out_specs=[vmem, vmem] + [any_space] * 4,
        scratch_shapes=[
            pltpu.VMEM((FFL, TILE), BF), pltpu.VMEM((FFL, TILE), BF), pltpu.VMEM((FFL, TILE), BF),
            pltpu.VMEM(rows, BF), pltpu.VMEM(rows, BF),
            pltpu.VMEM((4, 16, STEP), BF), pltpu.VMEM((8, 16, STEP), BF), pltpu.VMEM((XL, ROWS, TILE), F32),
            pltpu.VMEM((XL, 3, PART, CHUNK), F32), pltpu.VMEM((XL, 3, PART, CHUNK), F32), pltpu.VMEM((XL, 3, PART, CHUNK), F32),
            pltpu.VMEM((XL, 3, 2, PART, SUB), BF), pltpu.VMEM((XL, 3, 2, PART, SUB), BF),
            pltpu.VMEM((3, 2, PART, XL * CHUNK), BF), pltpu.VMEM((3, SUB, FFL), BF),
            pltpu.VMEM((2, Y, ROWS, HALF), F32), pltpu.VMEM((2,) + rows, BF),
            pltpu.VMEM((2, XL, 2, 3, 4, ROWS, HALF), BF),
            pltpu.VMEM((2, XL, 2, 4, ROWS, HALF), F32), pltpu.VMEM((2, XL, 2, 4, ROWS, HALF), BF),
            pltpu.VMEM((2, XL, 2, 3, ROWS, HALF), BF),
            pltpu.VMEM((2, XL, ROWS, TILE), F32), pltpu.VMEM((ROWS, TILE), F32),
            pltpu.VMEM((8, 16, STEP), F32), pltpu.VMEM((4, 4 * TILE), F32),
            pltpu.VMEM((XL, 4, 16, STEP), BF), pltpu.VMEM((8, 16, STEP), BF), pltpu.VMEM((FFL, TILE), BF),
            sem((3,)), sem((4,)), sem((7,)), sem((7,)), sem, sem,
            sem((2, XL, 2, 3)), sem((2, XL, 2, 3)), sem((2, XL, 2, 6)), sem((2, XL, 2, 6)),
            sem((XL, 3)), sem((XL, 3)), sem((XL, 3, 2)), sem((XL, 3, 2)), sem((XL, 2, 2)), sem((XL, 2, 2)),
            sem((2, XL, 3, 3)), sem((2, XL, 3, 3)), sem((2, XL, 2, 3)), sem((2, XL, 2, 3)),
            sem, sem, sem((7,)), sem((7,)),
        ],
        compiler_params=pltpu.CompilerParams(
            collective_id=0, has_side_effects=True, vmem_limit_bytes=62 * 1024 * 1024
        ),
        cost_estimate=pl.CostEstimate(flops=flops, bytes_accessed=20 * 1024 * 1024, transcendentals=0),
    )(act, cot, gate_proj, up_proj, down_proj)


def finish(
    out, ig, down, feat, gate_delta, up_delta, out_to, ig_to, down_to, gate_to, up_to,
    out_v, ig_v, down_v, feat_v, gd_v, ud_v, gate_v, up_v, sem_in, sem_out,
):
    blocks = TILE // STEP
    cols = [pl.ds(j * STEP, STEP) for j in range(blocks)]
    load_gd = pltpu.make_async_copy(gate_delta, gd_v, sem_in.at[0])
    load_ud = pltpu.make_async_copy(up_delta, ud_v, sem_in.at[1])
    load_feat = [pltpu.make_async_copy(feat.at[:, at], feat_v.at[:, at], sem_in.at[2 + j]) for j, at in enumerate(cols)]
    passed = ((down, down_v, down_to), (out, out_v, out_to), (ig, ig_v, ig_to))
    load_rest = [pltpu.make_async_copy(src, via, sem_in.at[2 + blocks + i]) for i, (src, via, _) in enumerate(passed)]
    load_gd.start()
    for load in load_feat:
        load.start()
    load_ud.start()
    for load in load_rest:
        load.start()
    stores = []

    def store(src, dst):
        stores.append(pltpu.make_async_copy(src, dst, sem_out.at[len(stores)]))
        stores[-1].start()

    load_gd.wait()
    for j, at in enumerate(cols):
        load_feat[j].wait()
        gate_v[:, at] = dot(gd_v[...], feat_v[:, at]).astype(BF)
        store(gate_v.at[:, at], gate_to.at[:, at])
    load_ud.wait()
    for load, (_, via, dst) in zip(load_rest, passed):
        load.wait()
        store(via, dst)
    for at in cols:
        up_v[:, at] = dot(ud_v[...], feat_v[:, at]).astype(BF)
        store(up_v.at[:, at], up_to.at[:, at])
    for copy in stores:
        copy.wait()


def local(activations, cotangent, gate_proj, up_proj, down_proj):
    block_output, input_gradient, down_gradient, features, gate_delta, up_delta = forward_backward(
        activations, cotangent, gate_proj.T, up_proj.T, down_proj
    )
    any_space = pl.BlockSpec(memory_space=pl.ANY)
    like = jax.ShapeDtypeStruct
    width = XL * CHUNK
    block_output, input_gradient, down_gradient, gate_gradient, up_gradient = pl.pallas_call(
        finish,
        name="finish",
        out_shape=[like((ROWS, TILE), BF), like((4, 4 * TILE), BF)] + [like((FFL, TILE), BF)] * 3,
        in_specs=[any_space] * 6,
        out_specs=[any_space] * 5,
        scratch_shapes=[
            pltpu.VMEM((ROWS, TILE), BF), pltpu.VMEM((4, 4 * TILE), BF), pltpu.VMEM((FFL, TILE), BF),
            pltpu.VMEM((width, TILE), BF), pltpu.VMEM((FFL, width), BF), pltpu.VMEM((FFL, width), BF),
            pltpu.VMEM((FFL, TILE), BF), pltpu.VMEM((FFL, TILE), BF),
            pltpu.SemaphoreType.DMA((9,)), pltpu.SemaphoreType.DMA((11,)),
        ],
        compiler_params=pltpu.CompilerParams(vmem_limit_bytes=62 * 1024 * 1024),
    )(
        block_output, input_gradient, down_gradient, features.reshape(width, TILE),
        gate_delta.reshape(FFL, width), up_delta.reshape(FFL, width),
    )
    return block_output, input_gradient, gate_gradient.T, up_gradient.T, down_gradient


def solution(mesh):
    placed = (
        P(("wide", "narrow"), None),
        P("wide", "narrow"),
        P("narrow", "wide"),
        P("narrow", "wide"),
        P("wide", "narrow"),
    )
    return jax.shard_map(
        local,
        mesh=mesh,
        in_specs=placed,
        out_specs=(
            P("wide", "narrow"),
            P(("wide", "narrow"), None),
            P("narrow", "wide"),
            P("narrow", "wide"),
            P("wide", "narrow"),
        ),
        check_vma=False,
    )
```

```python
import jax
import jax.numpy as jnp
from jax import lax
from jax.experimental import pallas as pl
from jax.experimental.pallas import tpu as pltpu
from jax.sharding import PartitionSpec as P

MESH = pl.DeviceIdType.MESH
BF = jnp.bfloat16
F32 = jnp.float32

XL, Z, Y = 2, 4, 4
ROWS = 16
TILE = 2048
HALF = TILE // 2
FFL = 832
CHUNK = Z * Y * ROWS
SUB = CHUNK // 2
OWN = Z - 1
PART = FFL // 2
STEP = 512


def dot(a, b):
    return lax.dot_general(a, b, (((1,), (0,)), ((), ())), preferred_element_type=F32)


def dot_t(a, b):
    return lax.dot_general(a, b, (((1,), (1,)), ((), ())), preferred_element_type=F32)


def kernel(
    act, cot, wg_hbm, wu_hbm, wd_hbm,
    out_ref, ig_ref, down_hbm, f_hbm, gd_hbm, ud_hbm,
    wg, wu, wd, feat, cota, a_send, a_recv, a_f32,
    g_send, g_own, g_recv, x_send, x_recv, hd, ht,
    part, r1_send, r1_recv, s1, r2_send, r2_recv, xo_send, xo_recv, t_f32, o_f32, n_send, n_recv, grad,
    w_sem, o_sem, a_ss, a_rs, cx_ss, cx_rs, p1_ss, p1_rs, p2_ss, p2_rs,
    g_ss, g_rs, x_ss, x_rs, h_ss, h_rs, r1_ss, r1_rs, r2_ss, r2_rs, xo_ss, xo_rs, n_ss, n_rs,
):
    w = lax.axis_index("wide")
    n = lax.axis_index("narrow")
    y = lax.rem(w, Y)
    z = lax.rem(w // Y, Z)
    xl = w // (Y * Z)
    xh = n // 2
    core = lax.rem(n, 2)

    def wide_id(a, b, c):
        return (a * Z + b) * Y + c

    def y_dev(d):
        return (wide_id(xl, z, lax.rem(y + d, Y)), n)

    def z_dev(d):
        return (wide_id(xl, lax.rem(z + d, Z), y), n)

    def line_dev(dx, dn):
        return (wide_id(lax.rem(xl + dx, XL), z, y), lax.rem(n + dn, 4))

    sibling = (w, xh * 2 + (1 - core))
    across = (w, (1 - xh) * 2 + core)
    peer = (wide_id(1 - xl, z, y), n)
    line = [(dx, dn) for dx in range(XL) for dn in range(4) if (dx, dn) != (0, 0)]

    sends = []

    def remote(src, dst, ss, rs, dev):
        return pltpu.make_async_remote_copy(
            src_ref=src, dst_ref=dst, send_sem=ss, recv_sem=rs, device_id=dev, device_id_type=MESH
        )

    def send(src, dst, ss, rs, dev):
        copy = remote(src, dst, ss, rs, dev)
        copy.start()
        sends.append(copy)

    def landed(dst, ss, rs, dev):
        remote(dst, dst, ss, rs, dev).wait_recv()

    loads = [
        pltpu.make_async_copy(src, dst, w_sem.at[i])
        for i, (src, dst) in enumerate(((wg_hbm, wg), (wu_hbm, wu), (wd_hbm, wd)))
    ]
    for load in loads:
        load.start()

    barrier = pltpu.get_barrier_semaphore()
    friends = [y_dev(d) for d in (1, 2, 3)] + [z_dev(d) for d in (1, 2, 3)] + [line_dev(*k) for k in line]
    for dev in friends:
        pl.semaphore_signal(barrier, inc=1, device_id=dev, device_id_type=MESH)

    rows4 = act[...].astype(F32)
    for m in range(4):
        for k in range(4):
            at = m * TILE + k * STEP
            t_f32[m, pl.ds(4 * k, 4), :] = rows4[:, at : at + STEP]
    for m in range(4):
        a_send[m] = t_f32[m].astype(BF)
    cota[0, OWN, y] = cot[...]

    pl.semaphore_wait(barrier, len(friends))

    def exchange(dx):
        for i, (ex, dn) in enumerate(line):
            if ex == dx:
                send(a_send.at[lax.rem(n + dn, 4)], a_recv.at[4 * dx + n], a_ss.at[i], a_rs.at[i], line_dev(dx, dn))

    def assemble(dx):
        for i, (ex, dn) in enumerate(line):
            if ex == dx:
                landed(a_recv.at[4 * dx + lax.rem(n + 4 - dn, 4)], a_ss.at[i], a_rs.at[i], line_dev(dx, dn))
        for m in range(4):
            t_f32[m] = a_recv[4 * dx + m].astype(F32)
            for k in range(4):
                a_f32[dx, pl.ds(4 * m, 4), pl.ds(k * STEP, STEP)] = t_f32[m, pl.ds(4 * k, 4), :]
        feat[dx, OWN, y] = a_f32[dx].astype(BF)

    bufs = (feat, cota)
    cols = (pl.ds(0, HALF), pl.ds(HALF, HALF))

    def gather1(b, c):
        block = [bufs[b].at[c, OWN, y, :, cols[h]] for h in (0, 1)]
        for d in (1, 2, 3):
            send(block[0], bufs[b].at[c, OWN - d, y, :, cols[0]], p1_ss.at[b, c, 0, d - 1], p1_rs.at[b, c, 0, d - 1], z_dev(d))
            send(block[1], block[1], p1_ss.at[b, c, 1, d - 1], p1_rs.at[b, c, 1, d - 1], y_dev(d))

    def gather1_wait(b, c):
        for d in (1, 2, 3):
            landed(bufs[b].at[c, OWN - d, y, :, cols[0]], p1_ss.at[b, c, 0, d - 1], p1_rs.at[b, c, 0, d - 1], z_dev(d))
            landed(bufs[b].at[c, OWN, lax.rem(y + 4 - d, Y), :, cols[1]], p1_ss.at[b, c, 1, d - 1], p1_rs.at[b, c, 1, d - 1], y_dev(d))

    low, high = pl.ds(0, 2), pl.ds(2, 2)

    def ring_block(b, c, h, back, part_of):
        if h == 0:
            return bufs[b].at[c, part_of, lax.rem(y + 4 - back, Y), :, cols[0]]
        return bufs[b].at[c, OWN - back, part_of, :, cols[1]]

    def ring_block_at(b, c, h, back, part_of, d):
        return ring_block(b, c, h, back if h == 0 else (back + d) % 4, part_of)

    def ring_dev(h, d):
        return y_dev(d) if h == 0 else z_dev(d)

    def gather2(b, c):
        for i, (d, part_of) in enumerate(((1, low), (3, high), (1, high), (3, low))):
            for h in (0, 1):
                block, there = ring_block(b, c, h, 0, part_of), ring_block_at(b, c, h, 0, part_of, d)
                send(block, there, p2_ss.at[b, c, h, i], p2_rs.at[b, c, h, i], ring_dev(h, d))

    def gather2_direct(b, c):
        for d in (1, 2, 3):
            for h in (0, 1):
                block, there = ring_block(b, c, h, 0, pl.ds(0, 4)), ring_block_at(b, c, h, 0, pl.ds(0, 4), d)
                send(block, there, p2_ss.at[b, c, h, d - 1], p2_rs.at[b, c, h, d - 1], ring_dev(h, d))

    def gather2_direct_wait(b, c):
        for d in (1, 2, 3):
            for h in (0, 1):
                landed(ring_block(b, c, h, d, pl.ds(0, 4)), p2_ss.at[b, c, h, d - 1], p2_rs.at[b, c, h, d - 1], ring_dev(h, d))

    def gather2_pass_on(b, c):
        for i, (d, part_of) in enumerate(((1, low), (3, high))):
            for h in (0, 1):
                block, there = ring_block(b, c, h, d, part_of), ring_block_at(b, c, h, d, part_of, d)
                landed(block, p2_ss.at[b, c, h, i], p2_rs.at[b, c, h, i], ring_dev(h, d))
                send(block, there, p2_ss.at[b, c, h, 4 + i], p2_rs.at[b, c, h, 4 + i], ring_dev(h, d))

    def gather2_wait(b, c):
        for i, (d, back, part_of) in ((2, (1, 1, high)), (3, (3, 3, low)), (4, (1, 2, low)), (5, (3, 2, high))):
            for h in (0, 1):
                landed(ring_block(b, c, h, back, part_of), p2_ss.at[b, c, h, i], p2_rs.at[b, c, h, i], ring_dev(h, d))

    def partial(c, core_of, k, into):
        rows = pl.ds(pl.multiple_of(PART * core_of, PART), PART)
        into[c, k] = dot_t((wg, wu, wd)[k][rows, :], (feat, feat, cota)[k][c].reshape(CHUNK, TILE))

    def sum_send(c, k):
        partial(c, 1 - core, k, g_send)
        send(g_send.at[c, k], g_recv.at[c, k], g_ss.at[c, k], g_rs.at[c, k], sibling)

    def sum_own(c, k):
        partial(c, core, k, g_own)

    subs = (pl.ds(0, SUB), pl.ds(SUB, SUB))

    def sum_chip(c, k):
        landed(g_recv.at[c, k], g_ss.at[c, k], g_rs.at[c, k], sibling)
        v = g_own[c, k] + g_recv[c, k]
        g_own[c, k] = v
        for s in (0, 1):
            x_send[c, k, s] = v[:, s * SUB : (s + 1) * SUB].astype(BF)

    def sum_across(c, k, s):
        send(x_send.at[c, k, s], x_recv.at[c, k, s], x_ss.at[c, k, s], x_rs.at[c, k, s], across)

    def arrived(c, k, s):
        landed(x_recv.at[c, k, s], x_ss.at[c, k, s], x_rs.at[c, k, s], across)
        return g_own[c, k, :, subs[s]] + x_recv[c, k, s].astype(F32)

    def tokens(c, s):
        return pl.ds(c * CHUNK + s * SUB, SUB)

    def share(c, s, g):
        block = hd.at[pl.ds(*((0, 1), (1, 2))[g]), core, :, tokens(c, s)]
        send(block, block, h_ss.at[c, s, g], h_rs.at[c, s, g], sibling)

    def share_wait(c, s, g):
        block = hd.at[pl.ds(*((0, 1), (1, 2))[g]), 1 - core, :, tokens(c, s)]
        landed(block, h_ss.at[c, s, g], h_rs.at[c, s, g], sibling)

    def hidden(c, s):
        gate, up = arrived(c, 0, s), arrived(c, 1, s)
        g_own[c, 0, :, subs[s]] = gate
        g_own[c, 1, :, subs[s]] = up
        hd[0, core, :, tokens(c, s)] = (gate * lax.logistic(gate) * up).astype(BF)
        share(c, s, 0)

    def deltas(c, s):
        gate, up, back = g_own[c, 0, :, subs[s]], g_own[c, 1, :, subs[s]], arrived(c, 2, s)
        sigma = lax.logistic(gate)
        hd[1, core, :, tokens(c, s)] = (back * up * (sigma * (1.0 + gate * (1.0 - sigma)))).astype(BF)
        hd[2, core, :, tokens(c, s)] = (back * (gate * sigma)).astype(BF)
        share(c, s, 1)

    def product(k, c, s):
        share_wait(c, s, k)
        for i in ((0,), (1, 2))[k]:
            ht[i] = hd[i, :, :, tokens(c, s)].reshape(FFL, SUB).T
        zs = pl.ds(2 * s, 2)
        for h in (0, 1):
            if k == 0:
                v = dot(ht[0], wd[:, cols[h]])
            else:
                v = dot(ht[1], wg[:, cols[h]]) + dot(ht[2], wu[:, cols[h]])
            v = v.reshape(2, Y, ROWS, HALF)
            part[...] = v
            r1_send[k, c, zs, :, :, cols[h]] = v.astype(BF)
            if h == 0:
                for d in (1, 2, 3):
                    send(r1_send.at[k, c, zs, lax.rem(y + d, Y), :, cols[0]], r1_recv.at[k, c, 0, d - 1, zs], r1_ss.at[k, c, s, d - 1], r1_rs.at[k, c, s, d - 1], y_dev(d))
                s1[k, c, 0, zs] = part[:, y]
            else:
                for j in (2 * s, 2 * s + 1):
                    if j == OWN:
                        s1[k, c, 1] = part[1]
                    else:
                        send(r1_send.at[k, c, j, :, :, cols[1]], r1_recv.at[k, c, 1, j], r1_ss.at[k, c, 2, j], r1_rs.at[k, c, 2, j], z_dev(j + 1))

    def scatter_z(k, c, s):
        zs = pl.ds(2 * s, 2)
        own = s1[k, c, 0, zs]
        for d in (1, 2, 3):
            landed(r1_recv.at[k, c, 0, d - 1, zs], r1_ss.at[k, c, s, d - 1], r1_rs.at[k, c, s, d - 1], y_dev(d))
            own += r1_recv[k, c, 0, d - 1, zs].astype(F32)
        s1[k, c, 0, zs] = own
        r2_send[k, c, 0, zs] = own.astype(BF)
        for j in (2 * s, 2 * s + 1):
            if j != OWN:
                send(r2_send.at[k, c, 0, j], r2_recv.at[k, c, 0, j], r2_ss.at[k, c, 0, j], r2_rs.at[k, c, 0, j], z_dev(j + 1))

    def scatter_y(k, c):
        own = s1[k, c, 1]
        for j in (0, 1, 2):
            landed(r1_recv.at[k, c, 1, j], r1_ss.at[k, c, 2, j], r1_rs.at[k, c, 2, j], z_dev(j + 1))
            own += r1_recv[k, c, 1, j].astype(F32)
        s1[k, c, 1] = own
        r2_send[k, c, 1] = own.astype(BF)
        for d in (1, 2, 3):
            send(r2_send.at[k, c, 1, lax.rem(y + d, Y)], r2_recv.at[k, c, 1, d - 1], r2_ss.at[k, c, 1, d - 1], r2_rs.at[k, c, 1, d - 1], y_dev(d))

    def scattered(k, c):
        for h in (0, 1):
            own = s1[k, c, h, OWN if h == 0 else y]
            for d in (1, 2, 3):
                landed(r2_recv.at[k, c, h, d - 1], r2_ss.at[k, c, h, d - 1], r2_rs.at[k, c, h, d - 1], ring_dev(1 - h, d))
                own += r2_recv[k, c, h, d - 1].astype(F32)
            xo_send[k, c, :, cols[h]] = own

    def owners(c):
        for m in range(4):
            for k in range(4):
                t_f32[m, pl.ds(4 * k, 4), :] = xo_send[1, c, pl.ds(4 * m, 4), pl.ds(k * STEP, STEP)]
        for m in range(4):
            n_send[c, m] = t_f32[m].astype(BF)
        for i, (dx, dn) in enumerate(line):
            if dx == c:
                send(n_send.at[c, lax.rem(n + dn, 4)], n_recv.at[4 * c + n], n_ss.at[i], n_rs.at[i], line_dev(dx, dn))

    stores = []

    def store(src, dst):
        stores.append(pltpu.make_async_copy(src, dst, o_sem.at[len(stores)]))
        stores[-1].start()

    def down_gradient():
        def columns(j, carry):
            at = pl.ds(pl.multiple_of(j * STEP, STEP), STEP)
            right = cota[:, :, :, :, at].reshape(XL * CHUNK, STEP)
            grad[:, at] = dot(hd[0].reshape(FFL, XL * CHUNK), right).astype(BF)
            return carry

        lax.fori_loop(0, TILE // STEP, columns, 0)
        store(grad, down_hbm)

    def sent(upto):
        for copy in sends[:upto]:
            copy.wait_send()
        del sends[:upto]

    exchange(0)
    gather1(1, 0)
    exchange(1)
    send(cota.at[0, OWN, y], cota.at[1, OWN, y], cx_ss, cx_rs, peer)
    a_recv[n] = a_send[n]
    assemble(0)
    gather1(0, 0)
    gather1_wait(0, 0)
    gather2_direct(0, 0)
    gather1_wait(1, 0)
    gather2(1, 0)
    assemble(1)
    gather1(0, 1)
    landed(cota.at[1, OWN, y], cx_ss, cx_rs, peer)
    gather1(1, 1)
    for load in loads:
        load.wait()
    gather2_direct_wait(0, 0)
    sum_send(0, 0)
    sum_send(0, 1)
    sum_own(0, 0)
    gather2_pass_on(1, 0)
    gather1_wait(0, 1)
    gather2(0, 1)
    sum_chip(0, 0)
    sum_across(0, 0, 0)
    sum_own(0, 1)
    sum_chip(0, 1)
    sum_across(0, 1, 0)
    sum_across(0, 0, 1)
    sum_across(0, 1, 1)
    gather2_wait(1, 0)
    sum_send(0, 2)
    gather2_pass_on(0, 1)
    gather1_wait(1, 1)
    gather2(1, 1)
    sum_own(0, 2)
    sum_chip(0, 2)
    sum_across(0, 2, 0)
    sum_across(0, 2, 1)
    gather2_wait(0, 1)
    sum_send(1, 0)
    sum_send(1, 1)
    gather2_pass_on(1, 1)
    hidden(0, 0)
    sum_own(1, 0)
    product(0, 0, 0)
    sum_chip(1, 0)
    sum_across(1, 0, 0)
    sum_own(1, 1)
    sum_chip(1, 1)
    sum_across(1, 1, 0)
    sum_across(1, 0, 1)
    sum_across(1, 1, 1)
    hidden(0, 1)
    gather2_wait(1, 1)
    sum_send(1, 2)
    product(0, 0, 1)
    deltas(0, 0)
    sum_own(1, 2)
    sum_chip(1, 2)
    sum_across(1, 2, 0)
    sum_across(1, 2, 1)
    product(1, 0, 0)
    deltas(0, 1)
    scatter_z(0, 0, 0)
    product(1, 0, 1)
    scatter_z(0, 0, 1)
    scatter_y(0, 0)
    hidden(1, 0)
    product(0, 1, 0)
    hidden(1, 1)
    scatter_z(1, 0, 0)
    product(0, 1, 1)
    scatter_z(1, 0, 1)
    scatter_y(1, 0)
    deltas(1, 0)
    product(1, 1, 0)
    early = len(sends)
    deltas(1, 1)
    product(1, 1, 1)
    store(feat, f_hbm)
    store(hd.at[1], gd_hbm)
    store(hd.at[2], ud_hbm)
    scatter_z(0, 1, 0)
    scatter_z(0, 1, 1)
    scatter_y(0, 1)
    scattered(0, 0)
    scattered(1, 0)
    owners(0)
    scatter_z(1, 1, 0)
    scatter_z(1, 1, 1)
    scatter_y(1, 1)
    scattered(0, 1)
    send(xo_send.at[0, 1], xo_recv, xo_ss, xo_rs, peer)
    down_gradient()
    sent(early)
    scattered(1, 1)
    owners(1)
    landed(xo_recv, xo_ss, xo_rs, peer)
    out_ref[...] = (xo_send[0, 0] + xo_recv[...]).astype(BF)
    n_recv[n] = n_send[0, n]
    for i, (dx, dn) in enumerate(line):
        landed(n_recv.at[4 * dx + lax.rem(n + 4 - dn, 4)], n_ss.at[i], n_rs.at[i], line_dev(dx, dn))
    for m in range(4):
        t_f32[m] = n_recv[m].astype(F32) + n_recv[4 + m].astype(F32)
        for k in range(4):
            at = m * TILE + k * STEP
            o_f32[:, pl.ds(at, STEP)] = t_f32[m, pl.ds(4 * k, 4), :]
    ig_ref[...] = o_f32[...].astype(BF)

    sent(len(sends))
    for copy in stores:
        copy.wait()


def forward_backward(act, cot, gate_proj, up_proj, down_proj):
    any_space = pl.BlockSpec(memory_space=pl.ANY)
    vmem = pl.BlockSpec(memory_space=pltpu.VMEM)
    sem = pltpu.SemaphoreType.DMA
    rows = (XL, Z, Y, ROWS, TILE)
    like = jax.ShapeDtypeStruct
    flops = 2 * 7 * XL * Z * Y * ROWS * TILE * FFL
    return pl.pallas_call(
        kernel,
        name="ffn",
        out_shape=[
            like((ROWS, TILE), BF), like((4, 4 * TILE), BF),
            like((FFL, TILE), BF), like(rows, BF), like((2, PART, XL * CHUNK), BF), like((2, PART, XL * CHUNK), BF),
        ],
        in_specs=[vmem, vmem, any_space, any_space, any_space],
        out_specs=[vmem, vmem] + [any_space] * 4,
        scratch_shapes=[
            pltpu.VMEM((FFL, TILE), BF), pltpu.VMEM((FFL, TILE), BF), pltpu.VMEM((FFL, TILE), BF),
            pltpu.VMEM(rows, BF), pltpu.VMEM(rows, BF),
            pltpu.VMEM((4, 16, STEP), BF), pltpu.VMEM((8, 16, STEP), BF), pltpu.VMEM((XL, ROWS, TILE), F32),
            pltpu.VMEM((XL, 3, PART, CHUNK), F32), pltpu.VMEM((XL, 3, PART, CHUNK), F32), pltpu.VMEM((XL, 3, PART, CHUNK), F32),
            pltpu.VMEM((XL, 3, 2, PART, SUB), BF), pltpu.VMEM((XL, 3, 2, PART, SUB), BF),
            pltpu.VMEM((3, 2, PART, XL * CHUNK), BF), pltpu.VMEM((3, SUB, FFL), BF),
            pltpu.VMEM((2, Y, ROWS, HALF), F32), pltpu.VMEM((2,) + rows, BF),
            pltpu.VMEM((2, XL, 2, 3, 4, ROWS, HALF), BF),
            pltpu.VMEM((2, XL, 2, 4, ROWS, HALF), F32), pltpu.VMEM((2, XL, 2, 4, ROWS, HALF), BF),
            pltpu.VMEM((2, XL, 2, 3, ROWS, HALF), BF),
            pltpu.VMEM((2, XL, ROWS, TILE), F32), pltpu.VMEM((ROWS, TILE), F32),
            pltpu.VMEM((8, 16, STEP), F32), pltpu.VMEM((4, 4 * TILE), F32),
            pltpu.VMEM((XL, 4, 16, STEP), BF), pltpu.VMEM((8, 16, STEP), BF), pltpu.VMEM((FFL, TILE), BF),
            sem((3,)), sem((4,)), sem((7,)), sem((7,)), sem, sem,
            sem((2, XL, 2, 3)), sem((2, XL, 2, 3)), sem((2, XL, 2, 6)), sem((2, XL, 2, 6)),
            sem((XL, 3)), sem((XL, 3)), sem((XL, 3, 2)), sem((XL, 3, 2)), sem((XL, 2, 2)), sem((XL, 2, 2)),
            sem((2, XL, 3, 3)), sem((2, XL, 3, 3)), sem((2, XL, 2, 3)), sem((2, XL, 2, 3)),
            sem, sem, sem((7,)), sem((7,)),
        ],
        compiler_params=pltpu.CompilerParams(
            collective_id=0, has_side_effects=True, vmem_limit_bytes=62 * 1024 * 1024
        ),
        cost_estimate=pl.CostEstimate(flops=flops, bytes_accessed=20 * 1024 * 1024, transcendentals=0),
    )(act, cot, gate_proj, up_proj, down_proj)


def finish(
    out, ig, down, feat, gate_delta, up_delta, out_to, ig_to, down_to, gate_to, up_to,
    out_v, ig_v, down_v, feat_v, gd_v, ud_v, gate_v, up_v, sem_in, sem_out,
):
    blocks = TILE // STEP
    cols = [pl.ds(j * STEP, STEP) for j in range(blocks)]
    load_gd = pltpu.make_async_copy(gate_delta, gd_v, sem_in.at[0])
    load_ud = pltpu.make_async_copy(up_delta, ud_v, sem_in.at[1])
    load_feat = [pltpu.make_async_copy(feat.at[:, at], feat_v.at[:, at], sem_in.at[2 + j]) for j, at in enumerate(cols)]
    passed = ((down, down_v, down_to), (out, out_v, out_to), (ig, ig_v, ig_to))
    load_rest = [pltpu.make_async_copy(src, via, sem_in.at[2 + blocks + i]) for i, (src, via, _) in enumerate(passed)]
    load_gd.start()
    for load in load_feat:
        load.start()
    load_ud.start()
    for load in load_rest:
        load.start()
    stores = []

    def store(src, dst):
        stores.append(pltpu.make_async_copy(src, dst, sem_out.at[len(stores)]))
        stores[-1].start()

    load_gd.wait()
    for j, at in enumerate(cols):
        load_feat[j].wait()
        gate_v[:, at] = dot(gd_v[...], feat_v[:, at]).astype(BF)
        store(gate_v.at[:, at], gate_to.at[:, at])
    load_ud.wait()
    for load, (_, via, dst) in zip(load_rest, passed):
        load.wait()
        store(via, dst)
    for at in cols:
        up_v[:, at] = dot(ud_v[...], feat_v[:, at]).astype(BF)
        store(up_v.at[:, at], up_to.at[:, at])
    for copy in stores:
        copy.wait()


def local(activations, cotangent, gate_proj, up_proj, down_proj):
    block_output, input_gradient, down_gradient, features, gate_delta, up_delta = forward_backward(
        activations, cotangent, gate_proj.T, up_proj.T, down_proj
    )
    any_space = pl.BlockSpec(memory_space=pl.ANY)
    like = jax.ShapeDtypeStruct
    width = XL * CHUNK
    block_output, input_gradient, down_gradient, gate_gradient, up_gradient = pl.pallas_call(
        finish,
        name="finish",
        out_shape=[like((ROWS, TILE), BF), like((4, 4 * TILE), BF)] + [like((FFL, TILE), BF)] * 3,
        in_specs=[any_space] * 6,
        out_specs=[any_space] * 5,
        scratch_shapes=[
            pltpu.VMEM((ROWS, TILE), BF), pltpu.VMEM((4, 4 * TILE), BF), pltpu.VMEM((FFL, TILE), BF),
            pltpu.VMEM((width, TILE), BF), pltpu.VMEM((FFL, width), BF), pltpu.VMEM((FFL, width), BF),
            pltpu.VMEM((FFL, TILE), BF), pltpu.VMEM((FFL, TILE), BF),
            pltpu.SemaphoreType.DMA((9,)), pltpu.SemaphoreType.DMA((11,)),
        ],
        compiler_params=pltpu.CompilerParams(vmem_limit_bytes=62 * 1024 * 1024),
    )(
        block_output, input_gradient, down_gradient, features.reshape(width, TILE),
        gate_delta.reshape(FFL, width), up_delta.reshape(FFL, width),
    )
    return block_output, input_gradient, gate_gradient.T, up_gradient.T, down_gradient


def solution(mesh):
    placed = (
        P(("wide", "narrow"), None),
        P("wide", "narrow"),
        P("narrow", "wide"),
        P("narrow", "wide"),
        P("wide", "narrow"),
    )
    return jax.shard_map(
        local,
        mesh=mesh,
        in_specs=placed,
        out_specs=(
            P("wide", "narrow"),
            P(("wide", "narrow"), None),
            P("narrow", "wide"),
            P("narrow", "wide"),
            P("wide", "narrow"),
        ),
        check_vma=False,
    )
```
